256 devices in a mesh: row: 32 (over z, x), col: 8 (over y, core).
Axes of the slice: x: 4, y: 4, z: 8, core: 2. Of those that a mesh axis runs over, the one named last changes fastest.
Arguments:
- video: float32 [16384, 1024], P(('row', 'col')), may hold values from -0.6 to 0.6
- text: float32 [16384, 1024], P(('row', 'col')), may hold values from -0.6 to 0.6
- match_ids: int32 [16384], P(('row', 'col')), may hold values from 0 to 16383, as said below
- log_scale: float32 [1], replicated, may hold values from 2 to 2.7
- bias: float32 [1], replicated, may hold values from -8 to -4
Outputs:
- video_loss: float32 [16384], P(('row', 'col'))
- video_grad: float32 [16384, 1024], P(('row', 'col'))
- text_grad: float32 [16384, 1024], P(('row', 'col'))
The draws below stay inside these ranges and needn't reach their ends.
Inputs may be any that keep to these rules, and one draw needn't show every extreme that they name: `match_ids`: a video row index.
All inputs are finite; a program needn't handle non-finite values.
Results may differ from the reference program's by a relative error of at most 0.0003.
Values sent between devices are 32-bit elements; how exact they have to be, the bound alone decides.
A program may use at most 64 MiB of HBM per device.

```python
import math
import jax
import jax.numpy as jnp
from jax import lax

D = 1024
BATCH = 16384


def rough_rows(key):
    first, second = jax.random.split(key, 2)
    base = jax.random.normal(first, (BATCH, D), jnp.float32)
    spread = jnp.exp(jax.random.uniform(second, (BATCH, 1), jnp.float32, math.log(0.3), math.log(3.0)))
    mixed = base
    return jnp.clip(0.03 * spread * mixed, -0.6, 0.6)


def draw_video(key, part):
    key = jax.random.fold_in(key, 3)
    return rough_rows(key)


def draw_text(key, part):
    key = jax.random.fold_in(key, 5)
    return rough_rows(key)


def draw_match_ids(key, part):
    key = jax.random.fold_in(key, 7)
    first, second = jax.random.split(key)
    values = jax.random.randint(first, (BATCH,), 0, BATCH, jnp.int32)
    spot = jax.random.randint(second, (), 0, BATCH, jnp.int32)
    other = (spot + BATCH // 2) % BATCH
    places = jnp.arange(BATCH, dtype=jnp.int32)
    values = jnp.where(places == spot, BATCH - 1, values)
    values = jnp.where(places == other, 0, values)
    return values.astype(jnp.int32)


def setup_inputs(seed: int = 0) -> dict:
    key_of = jax.random.split(jax.random.key(seed), 6)
    return {
        "video": draw_video(jax.random.fold_in(key_of[5], 71), 0),
        "text": draw_text(jax.random.fold_in(key_of[5], 71), 0),
        "match_ids": draw_match_ids(jax.random.fold_in(key_of[5], 71), 0),
        "log_scale": jnp.clip(jax.random.uniform(key_of[3], (1,), jnp.float32, 2.0, 2.7), 2.0, 2.7),
        "bias": jnp.clip(jax.random.uniform(key_of[4], (1,), jnp.float32, -8.0, -4.0), -8.0, -4.0),
    }


EPS = 1e-06
HIGH = lax.Precision.HIGHEST

def unit_rows(emb):
    inv = lax.rsqrt(lax.optimization_barrier(jnp.sum(emb * emb, axis=1, keepdims=True)) + EPS)
    return (emb * inv, inv)

def back_rows(unit, inv, grad):
    return (grad - unit * lax.optimization_barrier(jnp.sum(unit * grad, axis=1, keepdims=True))) * inv

def reference(video, text, match_ids, log_scale, bias):
    video_unit, video_inv = unit_rows(video)
    text_unit, text_inv = unit_rows(text)
    scale = jnp.exp(log_scale[0])
    shift = bias[0]
    block = min(512, BATCH)
    while BATCH % block != 0:
        block = block // 2
    count = BATCH // block
    blocks = video_unit.reshape(count, block, D)

    def step(carry, item):
        vblock, number = item
        index = number * block + jnp.arange(block, dtype=jnp.int32)
        logits = scale * jnp.dot(vblock, text_unit.T, precision=HIGH, preferred_element_type=jnp.float32) + shift
        sign = jnp.where(match_ids[None, :] == index[:, None], 1.0, -1.0).astype(jnp.float32)
        margin = sign * logits
        loss = lax.optimization_barrier(jnp.sum(jax.nn.softplus(-margin), axis=1))
        weight = -scale * sign * jax.nn.sigmoid(-margin)
        vgrad = jnp.dot(weight, text_unit, precision=HIGH, preferred_element_type=jnp.float32)
        carry = carry + jnp.dot(weight.T, vblock, precision=HIGH, preferred_element_type=jnp.float32)
        return (carry, (loss, vgrad))
    start = jnp.zeros((BATCH, D), jnp.float32)
    tgrad, (loss, vgrad) = lax.scan(step, start, (blocks, jnp.arange(count, dtype=jnp.int32)))
    video_loss = loss.reshape(BATCH)
    video_grad = back_rows(video_unit, video_inv, vgrad.reshape(BATCH, D))
    text_grad = back_rows(text_unit, text_inv, tgrad)
    return (video_loss, video_grad, text_grad)
```

```python
import jax
import jax.numpy as jnp
from jax import lax
from jax.experimental import pallas as pl
from jax.experimental.pallas import tpu as pltpu
from jax.sharding import PartitionSpec as P

EPS = 1e-06
MESH = pl.DeviceIdType.MESH
F32 = jnp.float32
BF16 = jnp.bfloat16


def dot_nn(a, b):
    return lax.dot_general(a, b, (((1,), (0,)), ((), ())), preferred_element_type=F32)


def dot_nt(a, b):
    return lax.dot_general(a, b, (((1,), (1,)), ((), ())), preferred_element_type=F32)


def dot_tn(a, b):
    return lax.dot_general(a, b, (((0,), (0,)), ((), ())), preferred_element_type=F32)


def split(x):
    hi = x.astype(BF16)
    return hi, (x - hi.astype(F32)).astype(BF16)


def rows(start, size):
    if not isinstance(start, int):
        start = pl.multiple_of(start, size)
    return pl.ds(start, size)


def kernel(
    video_ref, text_ref, ids_ref, log_scale_ref, bias_ref,
    loss_ref, vgrad_ref, tgrad_ref,
    vf, tf, vh, vl, th, tl, w, vg, tg, recv_t, recv_v, recv_s, ids_slot, ids_vec, vidx, lacc, lrow, lrecv, inv_v, inv_t,
    t_send, t_recv, z_send, z_recv, s_send, s_recv, i_send, i_recv,
    rt_send, rt_recv, rz_send, rz_recv, rs_send, rs_recv, l_send, l_recv,
):
    row, col = lax.axis_index("row"), lax.axis_index("col")
    z, x, y, core = row // 4, row % 4, col // 2, col % 2
    diag = (x + y) % 4

    def at(x_, y_, z_, core_):
        return (z_ * 4 + x_, y_ * 2 + core_)

    xp, xm, yp, ym = (x + 1) % 4, (x + 3) % 4, (y + 1) % 4, (y + 3) % 4
    next_a = at(jnp.where(diag == 3, x, xp), jnp.where(diag == 3, yp, y), z, core)
    next_b = at(jnp.where(diag == 3, xp, x), jnp.where(diag == 3, y, yp), z, core)
    prev_a = at(jnp.where(diag == 0, x, xm), jnp.where(diag == 0, ym, y), z, core)
    prev_b = at(jnp.where(diag == 0, xm, x), jnp.where(diag == 0, y, ym), z, core)
    t_out = (next_a, prev_a, next_b, prev_b)
    t_back = (prev_a, next_a, prev_b, next_b)
    z_out = (at(x, y, (z + 1) % 8, core), at(x, y, (z + 7) % 8, core))
    z_back = (z_out[1], z_out[0])
    other = at(x, y, z, 1 - core)

    barrier = pltpu.get_barrier_semaphore()
    for peer in t_out:
        pl.semaphore_signal(barrier, inc=1, device_id=peer, device_id_type=MESH)
    pl.semaphore_signal(barrier, inc=1, device_id=other, device_id_type=MESH)
    for step in range(1, 8):
        for c in range(2):
            pl.semaphore_signal(barrier, inc=1, device_id=at(x, y, (z + step) % 8, c), device_id_type=MESH)

    def unit(ref, inv_ref):
        full = ref[...]
        inv = lax.rsqrt(jnp.sum(full * full, axis=1, keepdims=True) + EPS)
        inv_ref[...] = jnp.broadcast_to(inv, (64, 128))
        return full * inv

    tu = unit(text_ref, inv_t)
    tf[rows(896, 64), :] = tu
    hi, lo = split(tu)
    th[rows(896, 64), :] = hi
    tl[rows(896, 64), :] = lo
    vu = unit(video_ref, inv_v)
    hi, lo = split(vu)
    for half in range(2):
        vf[rows(768 + 128 * half, 32), :] = vu[32 * half : 32 * half + 32]
        vh[rows(768 + 128 * half, 32), :] = hi[32 * half : 32 * half + 32]
        vl[rows(768 + 128 * half, 32), :] = lo[32 * half : 32 * half + 32]

    def t_copy(way, tick, src, dst):
        return pltpu.make_async_remote_copy(
            src_ref=tf.at[rows(src, 16)], dst_ref=tf.at[rows(dst, 16)],
            send_sem=t_send.at[way], recv_sem=t_recv.at[way, tick],
            device_id=t_out[way], device_id_type=MESH,
        )

    def z_copy(way, tick, src, dst):
        return pltpu.make_async_remote_copy(
            src_ref=vf.at[rows(src, 16)], dst_ref=vf.at[rows(dst, 16)],
            send_sem=z_send.at[way], recv_sem=z_recv.at[way, tick],
            device_id=z_out[way], device_id_type=MESH,
        )

    def s_copy(way, tick, src):
        return pltpu.make_async_remote_copy(
            src_ref=vf.at[rows(src, 16)], dst_ref=vf.at[rows(src + 32, 16)],
            send_sem=s_send.at[way], recv_sem=s_recv.at[way, tick],
            device_id=other, device_id_type=MESH,
        )

    def i_copy(way, step, src):
        return pltpu.make_async_remote_copy(
            src_ref=src, dst_ref=ids_slot.at[way, step],
            send_sem=i_send.at[way], recv_sem=i_recv.at[way, step],
            device_id=t_out[way], device_id_type=MESH,
        )

    pl.semaphore_wait(barrier, 19)

    for way in range(4):
        i_copy(way, 0, ids_ref.at[way // 2]).start()
    for part in range(2):
        for way in range(4):
            t_copy(way, part, 896 + 32 * (way // 2) + 16 * part, 32 * way + 16 * part).start()
        for way in range(2):
            for q in (2 * part, 2 * part + 1):
                z_copy(way, q, 768 + 128 * (q // 2) + 16 * (q % 2), 128 * (q // 2) + 64 * way + 16 * (q % 2)).start()
    for q in range(4):
        s_copy(q // 2, 14 + q % 2, 768 + 128 * (q // 2) + 16 * (q % 2)).start()

    local = lax.broadcasted_iota(jnp.int32, (32, 128), 0)
    for hg in range(4):
        for half in range(2):
            for way in range(2):
                for who in range(2):
                    if hg < 3:
                        from_z = (z + (7 - hg if way == 0 else hg + 1)) % 8
                    else:
                        from_z = (z + 4 * way) % 8
                    from_core = core if who == 0 else 1 - core
                    base = ((from_z * 4 + x) * 8 + y * 2 + from_core) * 64 + 32 * half
                    vidx[rows(256 * hg + 128 * half + 64 * way + 32 * who, 32), :] = local + base
    lacc[...] = jnp.zeros_like(lacc)

    scale = jnp.exp(jnp.full((1, 128), log_scale_ref[0], F32))
    bias = jnp.full((1, 128), bias_ref[0], F32)
    lane = lax.broadcasted_iota(jnp.int32, (1, 128), 1)

    def t_split(start, size):
        hi, lo = split(tf[rows(start, size), :])
        th[rows(start, size), :] = hi
        tl[rows(start, size), :] = lo

    def v_split(start, size):
        hi, lo = split(vf[rows(start, size), :])
        vh[rows(start, size), :] = hi
        vl[rows(start, size), :] = lo

    def v_slot(tick, way):
        q = tick % 4
        return 256 * (tick // 4) + 128 * (q // 2) + 64 * way + 16 * (q % 2)

    def block(n):
        m = (n >= 1).astype(jnp.int32) + (n >= 4).astype(jnp.int32) + (n >= 9).astype(jnp.int32)
        r = n - m * m
        vb = jnp.where(r <= m, r, m)
        tb = jnp.where(r <= m, m, r - m - 1)
        vs, ts = rows(vb * 256, 256), rows(tb * 256, 256)
        dots = dot_nt(vh[vs, :], th[ts, :]) + (dot_nt(vh[vs, :], tl[ts, :]) + dot_nt(vl[vs, :], th[ts, :]))
        total = jnp.zeros((256, 128), F32)
        for half in range(2):
            logits = dots[:, 128 * half : 128 * half + 128] * scale + bias
            match = vidx[vs, :] == ids_vec[tb * 2 + half]
            q = jnp.where(match, -logits, logits)
            e = jnp.exp(q)
            u = 1.0 + e
            weight = (jnp.where(match, -scale, scale) * e) / u
            small = e * (1.0 - e * (0.5 - e * (1.0 / 3.0)))
            total = total + jnp.where(e < 1.0 / 64.0, small, jnp.log(u))
            hi, lo = split(weight)
            cols = pl.ds(pl.multiple_of((tb * 2 + half) * 128, 128), 128)
            for k in range(2):
                w[vb * 2 + k, 0, :, cols] = hi[128 * k : 128 * k + 128]
                w[vb * 2 + k, 1, :, cols] = lo[128 * k : 128 * k + 128]
        lacc[vs, :] += total

    def count(tick):
        done = 0
        for bound, more in ((4, 1), (8, 1), (9, 1), (10, 1), (12, 2), (13, 2), (14, 8)):
            done = done + jnp.where(tick >= bound, more, 0)
        return done

    @pl.loop(0, 15)
    def _(tick):
        part = tick % 2
        step = tick // 2
        base = 128 * step + 16 * part

        @pl.when(tick < 14)
        def _():
            for way in range(4):
                slot = base + 32 * way
                t_copy(way, tick, slot, slot).wait_recv()

                @pl.when(tick < 12)
                def _():
                    t_copy(way, tick + 2, slot, slot + 128).start()

                @pl.when((tick >= 12) & (part == way % 2))
                def _():
                    t_copy(way, 14, slot, 960 + 32 * (way // 2) + 16 * (way % 2)).start()

            @pl.when(part == 0)
            def _():
                for way in range(4):
                    i_copy(way, step, ids_slot.at[way, step]).wait_recv()

                    @pl.when(tick < 12)
                    def _():
                        i_copy(way, step + 1, ids_slot.at[way, step]).start()

                    if way % 2 == 0:

                        @pl.when(tick == 12)
                        def _():
                            i_copy(way, 7, ids_slot.at[way, step]).start()

                ids_vec[step] = jnp.where(
                    lane < 64,
                    jnp.where(lane < 32, ids_slot[0, step], ids_slot[1, step]),
                    jnp.where(lane < 96, ids_slot[2, step], ids_slot[3, step]),
                )

        @pl.when(tick == 14)
        def _():
            for way in range(4):
                slot = 960 + 32 * (way // 2) + 16 * (way % 2)
                t_copy(way, 14, slot, slot).wait_recv()
            for way in (0, 2):
                i_copy(way, 7, ids_slot.at[way, 7]).wait_recv()
            ids_vec[7] = jnp.where(
                lane < 64,
                jnp.where(lane < 32, ids_ref[0], ids_ref[1]),
                jnp.where(lane < 96, ids_slot[0, 7], ids_slot[2, 7]),
            )

        for way in range(2):

            @pl.when(tick < 12)
            def _():
                slot = v_slot(tick, way)
                z_copy(way, tick, slot, slot).wait_recv()

                @pl.when(tick < 8)
                def _():
                    z_copy(way, tick + 4, slot, slot + 256).start()

                @pl.when((tick >= 8) & ((tick % 4) // 2 == way))
                def _():
                    last = 768 + 128 * way + 64 + 16 * (tick % 2)
                    z_copy(way, 12 + tick % 2, slot, last).start()

                s_copy(way, tick, slot).start()

            @pl.when((tick == 12) | (tick == 13))
            def _():
                slot = 768 + 128 * way + 64 + 16 * (tick % 2)
                z_copy(way, tick, slot, slot).wait_recv()
                s_copy(way, tick, slot).start()

            @pl.when((tick >= 1) & (tick <= 12))
            def _():
                slot = v_slot(tick - 1, way)
                s_copy(way, tick - 1, slot).wait_recv()
                v_split(slot + 32, 16)

            @pl.when(tick >= 13)
            def _():
                slot = 768 + 128 * way + 64 + 16 * ((tick - 1) % 2)
                s_copy(way, tick - 1, slot).wait_recv()
                v_split(slot + 32, 16)

            @pl.when(tick < 12)
            def _():
                v_split(v_slot(tick, way), 16)

            @pl.when((tick == 12) | (tick == 13))
            def _():
                v_split(768 + 128 * way + 64 + 16 * (tick % 2), 16)

            @pl.when(tick == 0)
            def _():
                for part_ in range(2):
                    slot = 768 + 128 * way + 16 * part_
                    s_copy(way, 14 + part_, slot).wait_recv()
                    v_split(slot + 32, 16)

        @pl.when(tick < 14)
        def _():
            for way in range(4):
                t_split(base + 32 * way, 16)

        @pl.when(tick == 14)
        def _():
            t_split(960, 64)

        @pl.loop(count(tick - 1), count(tick))
        def _(n):
            block(n)

    def rt_copy(way, part, step, src, dst):
        return pltpu.make_async_remote_copy(
            src_ref=tg.at[rows(src, 16)], dst_ref=recv_t.at[rows(dst, 16)],
            send_sem=rt_send.at[way], recv_sem=rt_recv.at[way, part, step],
            device_id=t_back[way], device_id_type=MESH,
        )

    def rt_slot(way, part, step):
        return jnp.where(step == 0, 896, 128 * (step - 1)) + 32 * way + 16 * part

    def t_pump(step, part, first):
        for way in range(4):
            slot = 128 * (step - 1) + 32 * way + 16 * part
            if not first or way % 2 == part:
                rt_copy(way, part, step, slot, slot).wait_recv()
                tg[rows(slot, 16), :] += recv_t[rows(slot, 16), :]
            rt_copy(way, part, step - 1, slot, rt_slot(way, part, step - 1)).start()

    def rz_copy(way, half, step, src):
        return pltpu.make_async_remote_copy(
            src_ref=vg.at[rows(src, 32)], dst_ref=recv_v.at[step, half, way],
            send_sem=rz_send.at[way], recv_sem=rz_recv.at[way, half, step],
            device_id=z_back[way], device_id_type=MESH,
        )

    def rs_copy(hg, half, way):
        src = 256 * hg + 128 * half + 64 * way + 32
        return pltpu.make_async_remote_copy(
            src_ref=vg.at[rows(src, 32)], dst_ref=recv_s.at[hg, half, way],
            send_sem=rs_send.at[0], recv_sem=rs_recv.at[hg, half, way],
            device_id=other, device_id_type=MESH,
        )

    def z_pump(hg, half, with_recv):
        for way in range(2):
            slot = 256 * hg + 128 * half + 64 * way
            rs_copy(hg, half, way).wait_recv()
            if with_recv[way]:
                rz_copy(way, half, hg + 1, slot).wait_recv()
                vg[rows(slot, 32), :] += recv_s[hg, half, way] + recv_v[hg + 1, half, way]
            else:
                vg[rows(slot, 32), :] += recv_s[hg, half, way]
            rz_copy(way, half, hg, slot).start()

    def z_last(half):
        slot = 768 + 128 * half + 64
        rs_copy(3, half, 1).wait_recv()
        vg[rows(slot, 32), :] += recv_s[3, half, 1]
        rz_copy(half, half, 3, slot).start()

    def t_grad(g):
        cols = pl.ds(pl.multiple_of(g * 128, 128), 128)
        hi = w[:, 0, :, cols].reshape(1024, 128)
        lo = w[:, 1, :, cols].reshape(1024, 128)
        both = dot_tn(jnp.concatenate([hi, lo], axis=1), vh[...])
        tg[rows(g * 128, 128), :] = both[:128] + (both[128:] + dot_tn(hi, vl[...]))

    def v_grad(m):
        both = dot_nn(w[m].reshape(256, 1024), th[...])
        vg[rows(m * 128, 128), :] = both[:128] + (both[128:] + dot_nn(w[m, 0], tl[...]))

    def l_copy(hg, way, who, owner):
        slot = (hg * 2 + way) * 2 + who
        return pltpu.make_async_remote_copy(
            src_ref=lrow.at[hg], dst_ref=lrecv.at[slot],
            send_sem=l_send.at[0], recv_sem=l_recv.at[slot],
            device_id=owner, device_id_type=MESH,
        )

    def l_peers():
        peers = []
        for hg in range(4):
            for way in range(2):
                if hg < 3:
                    to_z = (z + (7 - hg if way == 0 else hg + 1)) % 8
                else:
                    to_z = (z + 4 * way) % 8
                for who in range(2):
                    if (hg, way, who) != (3, 0, 0):
                        peers.append((hg, way, who, at(x, y, to_z, core if who == 0 else 1 - core)))
        return peers

    @pl.loop(0, 8)
    def _(i):
        t_grad(7 - i)

        @pl.when(i == 0)
        def _():
            for way in range(4):
                part = way % 2
                src = 960 + 32 * (way // 2) + 16 * part
                rt_copy(way, part, 7, src, 768 + 32 * way + 16 * part).start()

        @pl.when(i == 1)
        def _():
            t_pump(7, 0, True)
            z_last(0)

        @pl.when(i >= 2)
        def _():
            t_pump(8 - i, 0, False)

        @pl.when(i == 2)
        def _():
            z_last(1)

        @pl.when(i == 3)
        def _():
            z_pump(2, 0, (True, False))

        @pl.when(i == 4)
        def _():
            z_pump(2, 1, (False, True))

        @pl.when(i >= 5)
        def _():
            z_pump(2 - (i - 3) // 2, (i - 3) % 2, (True, True))

        hg, half = 3 - i // 2, i % 2
        v_grad(2 * hg + half)
        for way in range(2):
            rs_copy(hg, half, way).start()

        @pl.when(i == 1)
        def _():
            t_pump(7, 1, True)

        @pl.when(i >= 2)
        def _():
            t_pump(8 - i, 1, False)

        @pl.when(i == 3)
        def _():
            for m in range(8):
                turned = jnp.transpose(lacc[rows(m * 128, 128), :])
                lrow[m // 2, m % 2 : m % 2 + 1, :] = jnp.sum(turned, axis=0, keepdims=True)
            for hg_, way, who, owner in l_peers():
                l_copy(hg_, way, who, owner).start()

    z_pump(0, 1, (True, True))

    loss = lrow[3][:, :32]
    for hg, way, who, owner in l_peers():
        l_copy(hg, way, who, owner).wait_recv()
        first = 64 * way + 32 * who
        loss = loss + lrecv[(hg * 2 + way) * 2 + who][:, first : first + 32]
    loss_ref[...] = loss

    for ring in range(2):
        for part in range(2):
            own = 896 + 32 * ring + 16 * part
            total = tg[rows(own, 16), :]
            for way in (2 * ring, 2 * ring + 1):
                slot = 896 + 32 * way + 16 * part
                rt_copy(way, part, 0, own, slot).wait_recv()
                total = total + recv_t[rows(slot, 16), :]
            u = tf[rows(own, 16), :]
            first = 32 * ring + 16 * part
            back = total - u * jnp.sum(u * total, axis=1, keepdims=True)
            tgrad_ref[rows(first, 16), :] = back * inv_t[rows(first, 16), :1]

    for half in range(2):
        own = 768 + 128 * half
        rs_copy(3, half, 0).wait_recv()
        total = vg[rows(own, 32), :] + recv_s[3, half, 0]
        for way in range(2):
            rz_copy(way, half, 0, own).wait_recv()
            total = total + recv_v[0, half, way]
        u = vf[rows(own, 32), :]
        back = total - u * jnp.sum(u * total, axis=1, keepdims=True)
        vgrad_ref[rows(32 * half, 32), :] = back * inv_v[rows(32 * half, 32), :1]

    def drain(ref, sem):
        pltpu.make_async_remote_copy(
            src_ref=ref, dst_ref=ref, send_sem=sem, recv_sem=sem, device_id=other, device_id_type=MESH
        ).wait_send()

    for way in range(4):
        drain(tf.at[rows(0, 240)], t_send.at[way])
        drain(tg.at[rows(0, 240)], rt_send.at[way])
        drain(ids_slot.at[way, pl.ds(0, 8 if way % 2 == 0 else 7)], i_send.at[way])
    for way in range(2):
        drain(vf.at[rows(0, 224)], z_send.at[way])
        drain(vf.at[rows(0, 256)], s_send.at[way])
        drain(vg.at[rows(0, 224)], rz_send.at[way])
    drain(vg.at[rows(0, 512)], rs_send.at[0])
    drain(lrecv.at[pl.ds(0, 15)], l_send.at[0])


def shards(video, text, match_ids, log_scale, bias):
    ids = jnp.tile(match_ids.reshape(2, 1, 32), (1, 1, 4))
    vmem = pl.BlockSpec(memory_space=pltpu.VMEM)
    smem = pl.BlockSpec(memory_space=pltpu.SMEM)
    dma = pltpu.SemaphoreType.DMA
    loss, vgrad, tgrad = pl.pallas_call(
        kernel,
        out_shape=(
            jax.ShapeDtypeStruct((2, 32), F32),
            jax.ShapeDtypeStruct((64, 1024), F32),
            jax.ShapeDtypeStruct((64, 1024), F32),
        ),
        in_specs=[vmem, vmem, vmem, smem, smem],
        out_specs=(vmem, vmem, vmem),
        scratch_shapes=[
            pltpu.VMEM((1024, 1024), F32),
            pltpu.VMEM((1024, 1024), F32),
            pltpu.VMEM((1024, 1024), BF16),
            pltpu.VMEM((1024, 1024), BF16),
            pltpu.VMEM((1024, 1024), BF16),
            pltpu.VMEM((1024, 1024), BF16),
            pltpu.VMEM((8, 2, 128, 1024), BF16),
            pltpu.VMEM((1024, 1024), F32),
            pltpu.VMEM((1024, 1024), F32),
            pltpu.VMEM((1024, 1024), F32),
            pltpu.VMEM((4, 2, 2, 32, 1024), F32),
            pltpu.VMEM((4, 2, 2, 32, 1024), F32),
            pltpu.VMEM((4, 8, 1, 128), jnp.int32),
            pltpu.VMEM((8, 1, 128), jnp.int32),
            pltpu.VMEM((1024, 128), jnp.int32),
            pltpu.VMEM((1024, 128), F32),
            pltpu.VMEM((4, 2, 128), F32),
            pltpu.VMEM((16, 2, 128), F32),
            pltpu.VMEM((64, 128), F32),
            pltpu.VMEM((64, 128), F32),
            dma((4,)), dma((4, 15)),
            dma((2,)), dma((2, 14)),
            dma((2,)), dma((2, 16)),
            dma((4,)), dma((4, 8)),
            dma((4,)), dma((4, 2, 8)),
            dma((2,)), dma((2, 2, 4)),
            dma((1,)), dma((4, 2, 2)),
            dma((1,)), dma((16,)),
        ],
        compiler_params=pltpu.CompilerParams(
            collective_id=0, has_side_effects=True, vmem_limit_bytes=56 * 2**20
        ),
        cost_estimate=pl.CostEstimate(flops=18 * 2**30, bytes_accessed=2**20, transcendentals=3 * 2**20),
    )(video, text, ids, log_scale, bias)
    return loss.reshape(64), vgrad, tgrad


def solution(mesh):
    return jax.shard_map(
        shards,
        mesh=mesh,
        in_specs=(P(("row", "col"), None), P(("row", "col"), None), P(("row", "col")), P(), P()),
        out_specs=(P(("row", "col")), P(("row", "col"), None), P(("row", "col"), None)),
        check_vma=False,
    )
```

```python
import jax
import jax.numpy as jnp
from jax import lax
from jax.experimental import pallas as pl
from jax.experimental.pallas import tpu as pltpu
from jax.sharding import PartitionSpec as P

EPS = 1e-06
MESH = pl.DeviceIdType.MESH
F32 = jnp.float32
BF16 = jnp.bfloat16


OWN = -1


def make_source():
    source = {}
    for way in range(4):
        first, part = way // 2, way % 2
        across = (2, 3) if first == 0 else (0, 1)
        for k in range(2):
            source[way, k] = (OWN, first, k)
            source[way, 2 + k] = (OWN, 1 - first, k)
        source[way, 4] = (way, part)
        source[way, 5] = (across[0], 0)
        source[way, 6] = (across[1], 0)
        source[way, 7] = (across[0], 1)
        source[way, 8] = (across[1], 1)
        source[way, 9] = (way, 2 + part)
        source[way, 10] = (across[0], 4)
        source[way, 11] = (across[1], 4)
        source[way, 12] = (way, 7 if part else 5)
        source[way, 13] = (way, 8 if part else 6)
        source[way, 14] = (way, 11 if part else 10)
    return source


SOURCE = make_source()


def children(slot):
    return [key for key, value in sorted(SOURCE.items(), key=lambda item: item[0][1]) if value == slot]


def identity(slot):
    if slot[0] == OWN:
        return (0, 0, slot[1], slot[2])
    dx, dy, half, part = identity(SOURCE[slot])
    step = 1 if slot[0] % 2 else 3
    if slot[0] < 2:
        return ((dx + step) % 4, dy, half, part)
    return (dx, (dy + step) % 4, half, part)


def text_row(slot):
    if slot[0] == OWN:
        return 896 + 32 * slot[1] + 16 * slot[2]
    way, tick = slot
    if tick == 14:
        return 960 + 16 * way
    return 128 * (tick // 2) + 32 * way + 16 * (tick % 2)


def dot_nn(a, b):
    return lax.dot_general(a, b, (((1,), (0,)), ((), ())), preferred_element_type=F32)


def dot_nt(a, b):
    return lax.dot_general(a, b, (((1,), (1,)), ((), ())), preferred_element_type=F32)


def dot_tn(a, b):
    return lax.dot_general(a, b, (((0,), (0,)), ((), ())), preferred_element_type=F32)


def split(x):
    hi = x.astype(BF16)
    return hi, (x - hi.astype(F32)).astype(BF16)


def rows(start, size):
    if not isinstance(start, int):
        start = pl.multiple_of(start, size)
    return pl.ds(start, size)


def kernel(
    video_ref, text_ref, ids_ref, log_scale_ref, bias_ref,
    loss_ref, vgrad_ref, tgrad_ref,
    vf, tf, vh, vl, th, tl, w, vg, tg, recv_t, recv_v, recv_s, ids_all, ids_vec, vidx, lacc, lrow, lrecv, inv_v, inv_t,
    t_send, t_recv, z_send, z_recv, s_send, s_recv, i_send, i_recv,
    rt_send, rt_recv, rz_send, rz_recv, rs_send, rs_recv, l_send, l_recv,
):
    row, col = lax.axis_index("row"), lax.axis_index("col")
    z, x, y, core = row // 4, row % 4, col // 2, col % 2

    def at(x_, y_, z_, core_):
        return (z_ * 4 + x_, y_ * 2 + core_)

    xp, xm, yp, ym = (x + 1) % 4, (x + 3) % 4, (y + 1) % 4, (y + 3) % 4
    t_out = (at(xp, y, z, core), at(xm, y, z, core), at(x, yp, z, core), at(x, ym, z, core))
    t_back = (t_out[1], t_out[0], t_out[3], t_out[2])
    line_x = tuple(at((x + d) % 4, y, z, core) for d in range(4))
    line_y = tuple(at(x, (y + d) % 4, z, core) for d in range(4))
    z_out = (at(x, y, (z + 1) % 8, core), at(x, y, (z + 7) % 8, core))
    z_back = (z_out[1], z_out[0])
    other = at(x, y, z, 1 - core)

    barrier = pltpu.get_barrier_semaphore()
    for peer in line_x[1:] + line_y[1:]:
        pl.semaphore_signal(barrier, inc=1, device_id=peer, device_id_type=MESH)
    pl.semaphore_signal(barrier, inc=1, device_id=other, device_id_type=MESH)
    for step in range(1, 8):
        for c in range(2):
            pl.semaphore_signal(barrier, inc=1, device_id=at(x, y, (z + step) % 8, c), device_id_type=MESH)

    def unit(ref, inv_ref):
        full = ref[...]
        inv = lax.rsqrt(jnp.sum(full * full, axis=1, keepdims=True) + EPS)
        inv_ref[...] = jnp.broadcast_to(inv, (64, 128))
        return full * inv

    tu = unit(text_ref, inv_t)
    tf[rows(896, 64), :] = tu
    hi, lo = split(tu)
    th[rows(896, 64), :] = hi
    tl[rows(896, 64), :] = lo
    vu = unit(video_ref, inv_v)
    hi, lo = split(vu)
    for half in range(2):
        vf[rows(768 + 128 * half, 32), :] = vu[32 * half : 32 * half + 32]
        vh[rows(768 + 128 * half, 32), :] = hi[32 * half : 32 * half + 32]
        vl[rows(768 + 128 * half, 32), :] = lo[32 * half : 32 * half + 32]

    def t_copy(slot):
        way, tick = slot
        return pltpu.make_async_remote_copy(
            src_ref=tf.at[rows(text_row(SOURCE[slot]), 16)], dst_ref=tf.at[rows(text_row(slot), 16)],
            send_sem=t_send.at[way], recv_sem=t_recv.at[way, tick],
            device_id=t_out[way], device_id_type=MESH,
        )

    def z_copy(way, tick, src, dst):
        return pltpu.make_async_remote_copy(
            src_ref=vf.at[rows(src, 16)], dst_ref=vf.at[rows(dst, 16)],
            send_sem=z_send.at[way], recv_sem=z_recv.at[way, tick],
            device_id=z_out[way], device_id_type=MESH,
        )

    def s_copy(way, tick, src):
        return pltpu.make_async_remote_copy(
            src_ref=vf.at[rows(src, 16)], dst_ref=vf.at[rows(src + 32, 16)],
            send_sem=s_send.at[way], recv_sem=s_recv.at[way, tick],
            device_id=other, device_id_type=MESH,
        )

    def ix_copy(d):
        return pltpu.make_async_remote_copy(
            src_ref=ids_ref, dst_ref=ids_all.at[0, (4 - d) % 4],
            send_sem=i_send.at[0], recv_sem=i_recv.at[0, (4 - d) % 4],
            device_id=line_x[d], device_id_type=MESH,
        )

    def iy_copy(d):
        return pltpu.make_async_remote_copy(
            src_ref=ids_all.at[0], dst_ref=ids_all.at[(4 - d) % 4],
            send_sem=i_send.at[1], recv_sem=i_recv.at[1, (4 - d) % 4],
            device_id=line_y[d], device_id_type=MESH,
        )

    pl.semaphore_wait(barrier, 21)

    for d in range(1, 4):
        ix_copy(d).start()
    ids_all[0, 0] = ids_ref[...]
    for part in range(2):
        for way in range(4):
            t_copy((way, part)).start()
        for way in range(2):
            for q in (2 * part, 2 * part + 1):
                z_copy(way, q, 768 + 128 * (q // 2) + 16 * (q % 2), 128 * (q // 2) + 64 * way + 16 * (q % 2)).start()
    for k in range(2, 4):
        for way in range(4):
            t_copy((way, k)).start()
    for q in range(4):
        s_copy(q // 2, 14 + q % 2, 768 + 128 * (q // 2) + 16 * (q % 2)).start()

    local = lax.broadcasted_iota(jnp.int32, (32, 128), 0)
    for hg in range(4):
        for half in range(2):
            for way in range(2):
                for who in range(2):
                    if hg < 3:
                        from_z = (z + (7 - hg if way == 0 else hg + 1)) % 8
                    else:
                        from_z = (z + 4 * way) % 8
                    from_core = core if who == 0 else 1 - core
                    base = ((from_z * 4 + x) * 8 + y * 2 + from_core) * 64 + 32 * half
                    vidx[rows(256 * hg + 128 * half + 64 * way + 32 * who, 32), :] = local + base
    lacc[...] = jnp.zeros_like(lacc)

    scale = jnp.exp(jnp.full((1, 128), log_scale_ref[0], F32))
    bias = jnp.full((1, 128), bias_ref[0], F32)
    lane = lax.broadcasted_iota(jnp.int32, (1, 128), 1)

    def t_split(start, size):
        hi, lo = split(tf[rows(start, size), :])
        th[rows(start, size), :] = hi
        tl[rows(start, size), :] = lo

    def v_split(start, size):
        hi, lo = split(vf[rows(start, size), :])
        vh[rows(start, size), :] = hi
        vl[rows(start, size), :] = lo

    def v_slot(tick, way):
        q = tick % 4
        return 256 * (tick // 4) + 128 * (q // 2) + 64 * way + 16 * (q % 2)

    def block(n):
        m = (n >= 1).astype(jnp.int32) + (n >= 4).astype(jnp.int32) + (n >= 9).astype(jnp.int32)
        r = n - m * m
        vb = jnp.where(r <= m, r, m)
        tb = jnp.where(r <= m, m, r - m - 1)
        vs, ts = rows(vb * 256, 256), rows(tb * 256, 256)
        dots = dot_nt(vh[vs, :], th[ts, :]) + (dot_nt(vh[vs, :], tl[ts, :]) + dot_nt(vl[vs, :], th[ts, :]))
        total = jnp.zeros((256, 128), F32)
        for half in range(2):
            logits = dots[:, 128 * half : 128 * half + 128] * scale + bias
            match = vidx[vs, :] == ids_vec[tb * 2 + half]
            q = jnp.where(match, -logits, logits)
            e = jnp.exp(q)
            u = 1.0 + e
            weight = (jnp.where(match, -scale, scale) * e) / u
            small = e * (1.0 - e * (0.5 - e * (1.0 / 3.0)))
            total = total + jnp.where(e < 1.0 / 64.0, small, jnp.log(u))
            hi, lo = split(weight)
            cols = pl.ds(pl.multiple_of((tb * 2 + half) * 128, 128), 128)
            for k in range(2):
                w[vb * 2 + k, 0, :, cols] = hi[128 * k : 128 * k + 128]
                w[vb * 2 + k, 1, :, cols] = lo[128 * k : 128 * k + 128]
        lacc[vs, :] += total

    def group_ids(group):
        vec = jnp.zeros((1, 128), jnp.int32)
        for place in range(8):
            if group < 7:
                slot = (place // 2, 2 * group + place % 2)
            elif place < 4:
                slot = (OWN, place // 2, place % 2)
            else:
                slot = (place - 4, 14)
            dx, dy, half, part = identity(slot)
            ids = ids_all[dy, dx, pl.ds(2 * half + part, 1), :]
            vec = ids if place == 0 else jnp.where(lane < 16 * place, vec, ids)
        return vec

    def count(tick):
        done = 0
        for bound, more in ((4, 1), (8, 1), (9, 1), (10, 1), (12, 2), (13, 2), (14, 8)):
            done = done + jnp.where(tick >= bound, more, 0)
        return done

    @pl.loop(0, 15)
    def _(tick):
        base = 128 * (tick // 2) + 16 * (tick % 2)

        for k in range(15):

            @pl.when(tick == k)
            def _():
                for way in range(4):
                    t_copy((way, k)).wait_recv()
                    for child in children((way, k)):
                        t_copy(child).start()
                if k == 0:
                    for d in range(1, 4):
                        ix_copy(d).wait_recv()
                    for d in range(1, 4):
                        iy_copy(d).start()
                if k == 3:
                    for d in range(1, 4):
                        iy_copy(d).wait_recv()
                    for group in range(8):
                        ids_vec[group] = group_ids(group)

        for way in range(2):

            @pl.when(tick < 12)
            def _():
                slot = v_slot(tick, way)
                z_copy(way, tick, slot, slot).wait_recv()

                @pl.when(tick < 8)
                def _():
                    z_copy(way, tick + 4, slot, slot + 256).start()

                @pl.when((tick >= 8) & ((tick % 4) // 2 == way))
                def _():
                    last = 768 + 128 * way + 64 + 16 * (tick % 2)
                    z_copy(way, 12 + tick % 2, slot, last).start()

                s_copy(way, tick, slot).start()

            @pl.when((tick == 12) | (tick == 13))
            def _():
                slot = 768 + 128 * way + 64 + 16 * (tick % 2)
                z_copy(way, tick, slot, slot).wait_recv()
                s_copy(way, tick, slot).start()

            @pl.when((tick >= 1) & (tick <= 12))
            def _():
                slot = v_slot(tick - 1, way)
                s_copy(way, tick - 1, slot).wait_recv()
                v_split(slot + 32, 16)

            @pl.when(tick >= 13)
            def _():
                slot = 768 + 128 * way + 64 + 16 * ((tick - 1) % 2)
                s_copy(way, tick - 1, slot).wait_recv()
                v_split(slot + 32, 16)

            @pl.when(tick < 12)
            def _():
                v_split(v_slot(tick, way), 16)

            @pl.when((tick == 12) | (tick == 13))
            def _():
                v_split(768 + 128 * way + 64 + 16 * (tick % 2), 16)

            @pl.when(tick == 0)
            def _():
                for part_ in range(2):
                    slot = 768 + 128 * way + 16 * part_
                    s_copy(way, 14 + part_, slot).wait_recv()
                    v_split(slot + 32, 16)

        @pl.when(tick < 14)
        def _():
            for way in range(4):
                t_split(base + 32 * way, 16)

        @pl.when(tick == 14)
        def _():
            t_split(960, 64)

        @pl.loop(count(tick - 1), count(tick))
        def _(n):
            block(n)

    def rt_copy(slot):
        way, tick = slot
        row_ = text_row(slot)
        return pltpu.make_async_remote_copy(
            src_ref=tg.at[rows(row_, 16)], dst_ref=recv_t.at[rows(row_, 16)],
            send_sem=rt_send.at[way], recv_sem=rt_recv.at[way, tick],
            device_id=t_back[way], device_id_type=MESH,
        )

    def t_sum(slot):
        total = tg[rows(text_row(slot), 16), :]
        for child in children(slot):
            rt_copy(child).wait_recv()
            total = total + recv_t[rows(text_row(child), 16), :]
        return total

    def t_pump(tick):
        for way in range(4):
            slot = (way, tick)
            if children(slot):
                tg[rows(text_row(slot), 16), :] = t_sum(slot)
            rt_copy(slot).start()

    def rz_copy(way, half, step, src):
        return pltpu.make_async_remote_copy(
            src_ref=vg.at[rows(src, 32)], dst_ref=recv_v.at[step, half, way],
            send_sem=rz_send.at[way], recv_sem=rz_recv.at[way, half, step],
            device_id=z_back[way], device_id_type=MESH,
        )

    def rs_copy(hg, half, way):
        src = 256 * hg + 128 * half + 64 * way + 32
        return pltpu.make_async_remote_copy(
            src_ref=vg.at[rows(src, 32)], dst_ref=recv_s.at[hg, half, way],
            send_sem=rs_send.at[0], recv_sem=rs_recv.at[hg, half, way],
            device_id=other, device_id_type=MESH,
        )

    def z_pump(hg, half, with_recv):
        for way in range(2):
            slot = 256 * hg + 128 * half + 64 * way
            rs_copy(hg, half, way).wait_recv()
            if with_recv[way]:
                rz_copy(way, half, hg + 1, slot).wait_recv()
                vg[rows(slot, 32), :] += recv_s[hg, half, way] + recv_v[hg + 1, half, way]
            else:
                vg[rows(slot, 32), :] += recv_s[hg, half, way]
            rz_copy(way, half, hg, slot).start()

    def z_last(half):
        slot = 768 + 128 * half + 64
        rs_copy(3, half, 1).wait_recv()
        vg[rows(slot, 32), :] += recv_s[3, half, 1]
        rz_copy(half, half, 3, slot).start()

    def t_grad(g):
        cols = pl.ds(pl.multiple_of(g * 128, 128), 128)
        hi = w[:, 0, :, cols].reshape(1024, 128)
        lo = w[:, 1, :, cols].reshape(1024, 128)
        both = dot_tn(jnp.concatenate([hi, lo], axis=1), vh[...])
        tg[rows(g * 128, 128), :] = both[:128] + (both[128:] + dot_tn(hi, vl[...]))

    def v_grad(m):
        both = dot_nn(w[m].reshape(256, 1024), th[...])
        vg[rows(m * 128, 128), :] = both[:128] + (both[128:] + dot_nn(w[m, 0], tl[...]))

    def l_copy(hg, way, who, owner):
        slot = (hg * 2 + way) * 2 + who
        return pltpu.make_async_remote_copy(
            src_ref=lrow.at[hg], dst_ref=lrecv.at[slot],
            send_sem=l_send.at[0], recv_sem=l_recv.at[slot],
            device_id=owner, device_id_type=MESH,
        )

    def l_peers():
        peers = []
        for hg in range(4):
            for way in range(2):
                if hg < 3:
                    to_z = (z + (7 - hg if way == 0 else hg + 1)) % 8
                else:
                    to_z = (z + 4 * way) % 8
                for who in range(2):
                    if (hg, way, who) != (3, 0, 0):
                        peers.append((hg, way, who, at(x, y, to_z, core if who == 0 else 1 - core)))
        return peers

    @pl.loop(0, 8)
    def _(i):
        t_grad(7 - i)

        for k in range(8):

            @pl.when(i == k)
            def _():
                t_pump(14 if k == 0 else 15 - 2 * k)

        @pl.when(i == 1)
        def _():
            z_last(0)

        @pl.when(i == 2)
        def _():
            z_last(1)

        @pl.when(i == 3)
        def _():
            z_pump(2, 0, (True, False))

        @pl.when(i == 4)
        def _():
            z_pump(2, 1, (False, True))

        @pl.when(i >= 5)
        def _():
            z_pump(2 - (i - 3) // 2, (i - 3) % 2, (True, True))

        hg, half = 3 - i // 2, i % 2
        v_grad(2 * hg + half)
        for way in range(2):
            rs_copy(hg, half, way).start()

        for k in range(1, 8):

            @pl.when(i == k)
            def _():
                t_pump(14 - 2 * k)

        @pl.when(i == 3)
        def _():
            for m in range(8):
                turned = jnp.transpose(lacc[rows(m * 128, 128), :])
                lrow[m // 2, m % 2 : m % 2 + 1, :] = jnp.sum(turned, axis=0, keepdims=True)
            for hg_, way, who, owner in l_peers():
                l_copy(hg_, way, who, owner).start()

    z_pump(0, 1, (True, True))

    loss = lrow[3][:, :32]
    for hg, way, who, owner in l_peers():
        l_copy(hg, way, who, owner).wait_recv()
        first = 64 * way + 32 * who
        loss = loss + lrecv[(hg * 2 + way) * 2 + who][:, first : first + 32]
    loss_ref[...] = loss

    for half in range(2):
        for part in range(2):
            own = text_row((OWN, half, part))
            total = t_sum((OWN, half, part))
            u = tf[rows(own, 16), :]
            first = 32 * half + 16 * part
            back = total - u * jnp.sum(u * total, axis=1, keepdims=True)
            tgrad_ref[rows(first, 16), :] = back * inv_t[rows(first, 16), :1]

    for half in range(2):
        own = 768 + 128 * half
        rs_copy(3, half, 0).wait_recv()
        total = vg[rows(own, 32), :] + recv_s[3, half, 0]
        for way in range(2):
            rz_copy(way, half, 0, own).wait_recv()
            total = total + recv_v[0, half, way]
        u = vf[rows(own, 32), :]
        back = total - u * jnp.sum(u * total, axis=1, keepdims=True)
        vgrad_ref[rows(32 * half, 32), :] = back * inv_v[rows(32 * half, 32), :1]

    def drain(ref, sem):
        pltpu.make_async_remote_copy(
            src_ref=ref, dst_ref=ref, send_sem=sem, recv_sem=sem, device_id=other, device_id_type=MESH
        ).wait_send()

    for way in range(4):
        drain(tf.at[rows(0, 240)], t_send.at[way])
        drain(tg.at[rows(0, 240)], rt_send.at[way])
    for way in range(2):
        drain(vf.at[rows(0, 224)], z_send.at[way])
        drain(vf.at[rows(0, 256)], s_send.at[way])
        drain(vg.at[rows(0, 224)], rz_send.at[way])
    drain(ids_all.at[0, pl.ds(0, 3)], i_send.at[0])
    drain(ids_all.at[pl.ds(0, 3)], i_send.at[1])
    drain(vg.at[rows(0, 512)], rs_send.at[0])
    drain(lrecv.at[pl.ds(0, 15)], l_send.at[0])


def shards(video, text, match_ids, log_scale, bias):
    ids = jnp.tile(match_ids.reshape(4, 16), (1, 8))
    vmem = pl.BlockSpec(memory_space=pltpu.VMEM)
    smem = pl.BlockSpec(memory_space=pltpu.SMEM)
    dma = pltpu.SemaphoreType.DMA
    loss, vgrad, tgrad = pl.pallas_call(
        kernel,
        out_shape=(
            jax.ShapeDtypeStruct((2, 32), F32),
            jax.ShapeDtypeStruct((64, 1024), F32),
            jax.ShapeDtypeStruct((64, 1024), F32),
        ),
        in_specs=[vmem, vmem, vmem, smem, smem],
        out_specs=(vmem, vmem, vmem),
        scratch_shapes=[
            pltpu.VMEM((1024, 1024), F32),
            pltpu.VMEM((1024, 1024), F32),
            pltpu.VMEM((1024, 1024), BF16),
            pltpu.VMEM((1024, 1024), BF16),
            pltpu.VMEM((1024, 1024), BF16),
            pltpu.VMEM((1024, 1024), BF16),
            pltpu.VMEM((8, 2, 128, 1024), BF16),
            pltpu.VMEM((1024, 1024), F32),
            pltpu.VMEM((1024, 1024), F32),
            pltpu.VMEM((1024, 1024), F32),
            pltpu.VMEM((4, 2, 2, 32, 1024), F32),
            pltpu.VMEM((4, 2, 2, 32, 1024), F32),
            pltpu.VMEM((4, 4, 4, 128), jnp.int32),
            pltpu.VMEM((8, 1, 128), jnp.int32),
            pltpu.VMEM((1024, 128), jnp.int32),
            pltpu.VMEM((1024, 128), F32),
            pltpu.VMEM((4, 2, 128), F32),
            pltpu.VMEM((16, 2, 128), F32),
            pltpu.VMEM((64, 128), F32),
            pltpu.VMEM((64, 128), F32),
            dma((4,)), dma((4, 15)),
            dma((2,)), dma((2, 14)),
            dma((2,)), dma((2, 16)),
            dma((2,)), dma((2, 4)),
            dma((4,)), dma((4, 15)),
            dma((2,)), dma((2, 2, 4)),
            dma((1,)), dma((4, 2, 2)),
            dma((1,)), dma((16,)),
        ],
        compiler_params=pltpu.CompilerParams(
            collective_id=0, has_side_effects=True, vmem_limit_bytes=56 * 2**20
        ),
        cost_estimate=pl.CostEstimate(flops=18 * 2**30, bytes_accessed=2**20, transcendentals=3 * 2**20),
    )(video, text, ids, log_scale, bias)
    return loss.reshape(64), vgrad, tgrad


def solution(mesh):
    return jax.shard_map(
        shards,
        mesh=mesh,
        in_specs=(P(("row", "col"), None), P(("row", "col"), None), P(("row", "col")), P(), P()),
        out_specs=(P(("row", "col")), P(("row", "col"), None), P(("row", "col"), None)),
        check_vma=False,
    )
```

```python
import jax
import jax.numpy as jnp
from jax import lax
from jax.experimental import pallas as pl
from jax.experimental.pallas import tpu as pltpu
from jax.sharding import PartitionSpec as P

EPS = 1e-06
MESH = pl.DeviceIdType.MESH
F32 = jnp.float32
BF16 = jnp.bfloat16
F8 = jnp.float8_e4m3fn


OWN = -1


def make_source():
    source = {}
    for way in range(4):
        first, part = way // 2, way % 2
        across = (2, 3) if first == 0 else (0, 1)
        for k in range(2):
            source[way, k] = (OWN, first, k)
            source[way, 2 + k] = (OWN, 1 - first, k)
        source[way, 4] = (way, part)
        source[way, 5] = (across[0], 0)
        source[way, 6] = (across[1], 0)
        source[way, 7] = (across[0], 1)
        source[way, 8] = (across[1], 1)
        source[way, 9] = (way, 2 + part)
        source[way, 10] = (across[0], 4)
        source[way, 11] = (across[1], 4)
        source[way, 12] = (way, 7 if part else 5)
        source[way, 13] = (way, 8 if part else 6)
        source[way, 14] = (way, 11 if part else 10)
    return source


SOURCE = make_source()


def children(slot):
    return [key for key, value in sorted(SOURCE.items(), key=lambda item: item[0][1]) if value == slot]


def identity(slot):
    if slot[0] == OWN:
        return (0, 0, slot[1], slot[2])
    dx, dy, half, part = identity(SOURCE[slot])
    step = 1 if slot[0] % 2 else 3
    if slot[0] < 2:
        return ((dx + step) % 4, dy, half, part)
    return (dx, (dy + step) % 4, half, part)


def video_row(hg, half, way, who):
    if isinstance(hg, int) and hg == 3:
        return 768 + 128 * way + 64 * half + 32 * who
    return 256 * hg + 128 * half + 64 * way + 32 * who


def text_row(slot):
    if slot[0] == OWN:
        return 896 + 32 * slot[1] + 16 * slot[2]
    way, tick = slot
    if tick == 14:
        return 960 + 16 * way
    return 128 * (tick // 2) + 32 * way + 16 * (tick % 2)


def dot_nn(a, b):
    return lax.dot_general(a, b, (((1,), (0,)), ((), ())), preferred_element_type=F32)


def dot_nt(a, b):
    return lax.dot_general(a, b, (((1,), (1,)), ((), ())), preferred_element_type=F32)


def dot_tn(a, b):
    return lax.dot_general(a, b, (((0,), (0,)), ((), ())), preferred_element_type=F32)


def split(x):
    hi = x.astype(BF16)
    return hi, x - hi.astype(F32)


HI8, LO8 = 2.0**8, 2.0**17
W_HI8, W_LO8 = 2.0**4, 2.0**13


def rows(start, size):
    if not isinstance(start, int):
        start = pl.multiple_of(start, size)
    return pl.ds(start, size)


def kernel(
    video_any, text_any, ids_any, log_scale_any, bias_any,
    loss_ref, vgrad_ref, tgrad_ref,
    vf, tf, vh, v8, th, t8, dots, w, w8, vg, tg, recv_t, recv_v, recv_s, ids_all, ids_own, ids_vec, vidx, lacc, lrow, lrecv, inv_v, inv_t, video_ref, text_ref, ids_ref, log_scale_ref, bias_ref,
    t_send, t_recv, z_send, z_recv, s_send, s_recv, i_send, i_recv,
    rt_send, rt_recv, rz_send, rz_recv, rs_send, rs_recv, l_send, l_recv, in_sem,
):
    row, col = lax.axis_index("row"), lax.axis_index("col")
    z, x, y, core = row // 4, row % 4, col // 2, col % 2

    def at(x_, y_, z_, core_):
        return (z_ * 4 + x_, y_ * 2 + core_)

    xp, xm, yp, ym = (x + 1) % 4, (x + 3) % 4, (y + 1) % 4, (y + 3) % 4
    t_out = (at(xp, y, z, core), at(xm, y, z, core), at(x, yp, z, core), at(x, ym, z, core))
    t_back = (t_out[1], t_out[0], t_out[3], t_out[2])
    line_x = tuple(at((x + d) % 4, y, z, core) for d in range(4))
    line_y = tuple(at(x, (y + d) % 4, z, core) for d in range(4))
    z_out = (at(x, y, (z + 1) % 8, core), at(x, y, (z + 7) % 8, core))
    z_back = (z_out[1], z_out[0])
    other = at(x, y, z, 1 - core)

    loads = [
        pltpu.make_async_copy(src, dst, in_sem.at[n])
        for n, (src, dst) in enumerate(
            (
                (text_any, text_ref), (video_any, video_ref), (ids_any, ids_ref),
                (log_scale_any, log_scale_ref), (bias_any, bias_ref),
            )
        )
    ]
    for load in loads:
        load.start()

    barrier = pltpu.get_barrier_semaphore()
    for peer in line_x[1:] + line_y[1:]:
        pl.semaphore_signal(barrier, inc=1, device_id=peer, device_id_type=MESH)
    pl.semaphore_signal(barrier, inc=1, device_id=other, device_id_type=MESH)
    for step in range(1, 8):
        for c in range(2):
            pl.semaphore_signal(barrier, inc=1, device_id=at(x, y, (z + step) % 8, c), device_id_type=MESH)

    def unit(ref, inv_ref):
        full = ref[...]
        inv = lax.rsqrt(jnp.sum(full * full, axis=1, keepdims=True) + EPS)
        inv_ref[...] = jnp.broadcast_to(inv, (64, 128))
        return full * inv

    loads[0].wait()
    tu = unit(text_ref, inv_t)
    tf[rows(896, 64), :] = tu
    loads[1].wait()
    vu = unit(video_ref, inv_v)
    for half in range(2):
        vf[rows(768 + 64 * half, 32), :] = vu[32 * half : 32 * half + 32]
    lane = lax.broadcasted_iota(jnp.int32, (1, 128), 1)
    loads[2].wait()
    for quarter in range(4):
        vec = jnp.zeros((1, 128), jnp.int32)
        for n in range(16):
            vec = jnp.where(lane % 16 == n, ids_ref[16 * quarter + n], vec)
        ids_own[quarter : quarter + 1, :] = vec

    def t_copy(slot):
        way, tick = slot
        return pltpu.make_async_remote_copy(
            src_ref=tf.at[rows(text_row(SOURCE[slot]), 16)], dst_ref=tf.at[rows(text_row(slot), 16)],
            send_sem=t_send.at[way], recv_sem=t_recv.at[way, tick],
            device_id=t_out[way], device_id_type=MESH,
        )

    def z_copy(way, tick, src, dst):
        return pltpu.make_async_remote_copy(
            src_ref=vf.at[rows(src, 16)], dst_ref=vf.at[rows(dst, 16)],
            send_sem=z_send.at[way], recv_sem=z_recv.at[way, tick],
            device_id=z_out[way], device_id_type=MESH,
        )

    def s_copy(way, tick, src):
        return pltpu.make_async_remote_copy(
            src_ref=vf.at[rows(src, 16)], dst_ref=vf.at[rows(src + 32, 16)],
            send_sem=s_send.at[way], recv_sem=s_recv.at[way, tick],
            device_id=other, device_id_type=MESH,
        )

    def ix_copy(d):
        return pltpu.make_async_remote_copy(
            src_ref=ids_own, dst_ref=ids_all.at[0, (4 - d) % 4],
            send_sem=i_send.at[0], recv_sem=i_recv.at[0, (4 - d) % 4],
            device_id=line_x[d], device_id_type=MESH,
        )

    def iy_copy(d):
        return pltpu.make_async_remote_copy(
            src_ref=ids_all.at[0], dst_ref=ids_all.at[(4 - d) % 4],
            send_sem=i_send.at[1], recv_sem=i_recv.at[1, (4 - d) % 4],
            device_id=line_y[d], device_id_type=MESH,
        )

    pl.semaphore_wait(barrier, 21)

    for d in range(1, 4):
        ix_copy(d).start()
    ids_all[0, 0] = ids_own[...]
    for part in range(2):
        for way in range(4):
            t_copy((way, part)).start()
        for way in range(2):
            for q in (2 * part, 2 * part + 1):
                z_copy(way, q, 768 + 64 * (q // 2) + 16 * (q % 2), 128 * (q // 2) + 64 * way + 16 * (q % 2)).start()
    for k in range(2, 4):
        for way in range(4):
            t_copy((way, k)).start()
    for q in range(4):
        s_copy(q // 2, 14 + q % 2, 768 + 64 * (q // 2) + 16 * (q % 2)).start()

    local = lax.broadcasted_iota(jnp.int32, (32, 128), 0)
    for hg in range(4):
        for half in range(2):
            for way in range(2):
                for who in range(2):
                    if hg < 3:
                        from_z = (z + (7 - hg if way == 0 else hg + 1)) % 8
                    else:
                        from_z = (z + 4 * way) % 8
                    from_core = core if who == 0 else 1 - core
                    base = ((from_z * 4 + x) * 8 + y * 2 + from_core) * 64 + 32 * half
                    vidx[rows(video_row(hg, half, way, who), 32), :] = local + base
    lacc[...] = jnp.zeros_like(lacc)

    loads[3].wait()
    loads[4].wait()
    scale = jnp.exp(jnp.full((1, 128), log_scale_ref[0], F32))
    bias = jnp.full((1, 128), bias_ref[0], F32)

    def t_split(start, size):
        full = tf[rows(start, size), :]
        hi, lo = split(full)
        th[rows(start, size), :] = hi
        t8[0, rows(start, size), :] = (lo * LO8).astype(F8)
        t8[1, rows(start, size), :] = (full * HI8).astype(F8)

    def v_split(start, size):
        full = vf[rows(start, size), :]
        hi, lo = split(full)
        vh[rows(start, size), :] = hi
        v8[0, rows(start, size), :] = (full * HI8).astype(F8)
        v8[1, rows(start, size), :] = (lo * LO8).astype(F8)

    def v_slot(tick, way):
        q = tick % 4
        return 256 * (tick // 4) + 128 * (q // 2) + 64 * way + 16 * (q % 2)

    def place(n):
        if isinstance(n, int):
            m = int(n**0.5)
            r = n - m * m
            return (r, m) if r <= m else (m, r - m - 1)
        m = (n >= 1).astype(jnp.int32) + (n >= 4).astype(jnp.int32) + (n >= 9).astype(jnp.int32)
        r = n - m * m
        return jnp.where(r <= m, r, m), jnp.where(r <= m, m, r - m - 1)

    def block_dots(n):
        vb, tb = place(n)
        vs, ts = rows(vb * 256, 256), rows(tb * 256, 256)
        small = dot_nt(
            jnp.concatenate([v8[0, vs, :], v8[1, vs, :]], axis=1), jnp.concatenate([t8[0, ts, :], t8[1, ts, :]], axis=1)
        )
        dots[...] = dot_nt(vh[vs, :], th[ts, :]) + small * (1.0 / (HI8 * LO8))

    def block_rest(n):
        vb, tb = place(n)
        vs = rows(vb * 256, 256)
        total = jnp.zeros((256, 128), F32)
        for half in range(2):
            logits = dots[:, 128 * half : 128 * half + 128] * scale + bias
            match = vidx[vs, :] == ids_vec[tb * 2 + half]
            q = jnp.where(match, -logits, logits)
            e = jnp.exp(q)
            u = 1.0 + e
            weight = (jnp.where(match, -scale, scale) * e) / u
            small = e * (1.0 - e * (0.5 - e * (1.0 / 3.0)))
            total = total + jnp.where(e < 1.0 / 64.0, small, jnp.log(u))
            hi, lo = split(weight)
            hi8, lo8 = (weight * W_HI8).astype(F8), (lo * W_LO8).astype(F8)
            cols = rows((tb * 2 + half) * 128, 128)
            for k in range(2):
                w[vb * 2 + k, :, cols] = hi[128 * k : 128 * k + 128]
                w8[0, vb * 2 + k, :, cols] = hi8[128 * k : 128 * k + 128]
                w8[1, vb * 2 + k, :, cols] = lo8[128 * k : 128 * k + 128]
        lacc[vs, :] += total

    def group_ids(group):
        vec = jnp.zeros((1, 128), jnp.int32)
        for spot in range(8):
            if group < 7:
                slot = (spot // 2, 2 * group + spot % 2)
            elif spot < 4:
                slot = (OWN, spot // 2, spot % 2)
            else:
                slot = (spot - 4, 14)
            dx, dy, half, part = identity(slot)
            ids = ids_all[dy, dx, pl.ds(2 * half + part, 1), :]
            vec = ids if spot == 0 else jnp.where(lane < 16 * spot, vec, ids)
        return vec

    def count(tick):
        done = 0
        for bound, more in ((4, 1), (8, 1), (9, 1), (10, 1), (12, 2), (13, 2), (14, 8)):
            done = done + jnp.where(tick >= bound, more, 0)
        return done

    @pl.loop(0, 15)
    def _(tick):
        for k in range(15):

            @pl.when(tick == k)
            def _():
                for way in range(4):
                    t_copy((way, k)).wait_recv()
                    for child in children((way, k)):
                        t_copy(child).start()
                if k == 0:
                    for d in range(1, 4):
                        ix_copy(d).wait_recv()
                    for d in range(1, 4):
                        iy_copy(d).start()
                if k == 3:
                    for d in range(1, 4):
                        iy_copy(d).wait_recv()
                    for group in range(8):
                        ids_vec[group] = group_ids(group)

        for way in range(2):

            @pl.when(tick < 12)
            def _():
                slot = v_slot(tick, way)
                z_copy(way, tick, slot, slot).wait_recv()

                @pl.when(tick < 8)
                def _():
                    z_copy(way, tick + 4, slot, slot + 256).start()

                @pl.when((tick >= 8) & ((tick % 4) // 2 == way))
                def _():
                    last = 896 + 64 * way + 16 * (tick % 2)
                    z_copy(way, 12 + tick % 2, slot, last).start()

                s_copy(way, tick, slot).start()

            @pl.when((tick == 12) | (tick == 13))
            def _():
                slot = 896 + 64 * way + 16 * (tick % 2)
                z_copy(way, tick, slot, slot).wait_recv()
                s_copy(way, tick, slot).start()

            @pl.when((tick >= 1) & (tick <= 12))
            def _():
                s_copy(way, tick - 1, v_slot(tick - 1, way)).wait_recv()

            @pl.when(tick >= 13)
            def _():
                s_copy(way, tick - 1, 896 + 64 * way + 16 * ((tick - 1) % 2)).wait_recv()

            @pl.when(tick == 1)
            def _():
                for part in range(2):
                    s_copy(way, 14 + part, 768 + 64 * way + 16 * part).wait_recv()

        @pl.when(tick == 0)
        def _():
            t_split(896, 64)

        @pl.when(tick % 2 == 1)
        def _():
            t_split(128 * (tick // 2), 128)

        @pl.when((tick % 2 == 0) & (tick >= 2) & (tick <= 12))
        def _():
            v_split(128 * (tick // 2 - 1), 128)

        @pl.when(tick == 1)
        def _():
            v_split(768, 128)

        @pl.when(tick == 14)
        def _():
            v_split(896, 128)
            t_split(960, 64)

        @pl.when(tick == 4)
        def _():
            block_dots(0)

        @pl.loop(jnp.maximum(count(tick - 1), 1), count(tick))
        def _(n):
            block_rest(n - 1)
            block_dots(n)

    block_rest(15)

    def rt_copy(slot):
        way, tick = slot
        row_ = text_row(slot)
        return pltpu.make_async_remote_copy(
            src_ref=tg.at[rows(row_, 16)], dst_ref=recv_t.at[rows(row_, 16)],
            send_sem=rt_send.at[way], recv_sem=rt_recv.at[way, tick],
            device_id=t_back[way], device_id_type=MESH,
        )

    def t_sum(slot):
        total = tg[rows(text_row(slot), 16), :]
        for child in children(slot):
            rt_copy(child).wait_recv()
            total = total + recv_t[rows(text_row(child), 16), :]
        return total

    def t_pump(tick):
        for way in range(4):
            slot = (way, tick)
            if children(slot):
                tg[rows(text_row(slot), 16), :] = t_sum(slot)
            rt_copy(slot).start()

    def rz_copy(way, half, step, src):
        return pltpu.make_async_remote_copy(
            src_ref=vg.at[rows(src, 32)], dst_ref=recv_v.at[step, half, way],
            send_sem=rz_send.at[way], recv_sem=rz_recv.at[way, half, step],
            device_id=z_back[way], device_id_type=MESH,
        )

    def rs_copy(hg, half, way):
        return pltpu.make_async_remote_copy(
            src_ref=vg.at[rows(video_row(hg, half, way, 1), 32)], dst_ref=recv_s.at[hg, half, way],
            send_sem=rs_send.at[0], recv_sem=rs_recv.at[hg, half, way],
            device_id=other, device_id_type=MESH,
        )

    def z_pump(hg, half, with_recv):
        for way in range(2):
            slot = 256 * hg + 128 * half + 64 * way
            rs_copy(hg, half, way).wait_recv()
            if with_recv[way]:
                rz_copy(way, half, hg + 1, slot).wait_recv()
                vg[rows(slot, 32), :] += recv_s[hg, half, way] + recv_v[hg + 1, half, way]
            else:
                vg[rows(slot, 32), :] += recv_s[hg, half, way]
            rz_copy(way, half, hg, slot).start()

    def z_last():
        for half in range(2):
            slot = 896 + 64 * half
            rs_copy(3, half, 1).wait_recv()
            vg[rows(slot, 32), :] += recv_s[3, half, 1]
            rz_copy(half, half, 3, slot).start()

    def t_grad(g):
        cols = pl.ds(pl.multiple_of(g * 128, 128), 128)
        hi = w[:, :, cols].reshape(1024, 128)
        lo8 = w8[1, :, :, cols].reshape(1024, 128)
        hi8 = w8[0, :, :, cols].reshape(1024, 128)
        small = dot_tn(jnp.concatenate([lo8, hi8], axis=0), v8[...].reshape(2048, 1024))
        tg[rows(g * 128, 128), :] = dot_tn(hi, vh[...]) + small * (1.0 / (W_HI8 * LO8))

    def v_grad(m):
        small = dot_nn(jnp.concatenate([w8[0, m], w8[1, m]], axis=1), t8[...].reshape(2048, 1024))
        vg[rows(m * 128, 128), :] = dot_nn(w[m], th[...]) + small * (1.0 / (W_HI8 * LO8))

    def l_copy(hg, way, who, owner):
        slot = (hg * 2 + way) * 2 + who
        return pltpu.make_async_remote_copy(
            src_ref=lrow.at[hg], dst_ref=lrecv.at[slot],
            send_sem=l_send.at[0], recv_sem=l_recv.at[slot],
            device_id=owner, device_id_type=MESH,
        )

    def l_peers():
        peers = []
        for hg in range(4):
            for way in range(2):
                if hg < 3:
                    to_z = (z + (7 - hg if way == 0 else hg + 1)) % 8
                else:
                    to_z = (z + 4 * way) % 8
                for who in range(2):
                    if (hg, way, who) != (3, 0, 0):
                        peers.append((hg, way, who, at(x, y, to_z, core if who == 0 else 1 - core)))
        return peers

    t_grad(7)
    t_pump(14)

    @pl.loop(0, 7)
    def _(i):
        hg, half = 2 - (i - 1) // 2, (i - 1) % 2
        v_grad(jnp.where(i == 0, 7, 2 * hg + half))

        @pl.when(i == 0)
        def _():
            for half_ in range(2):
                rs_copy(3, half_, 1).start()

        @pl.when(i > 0)
        def _():
            for way in range(2):
                rs_copy(hg, half, way).start()

        t_grad(6 - i)
        for k in range(7):

            @pl.when(i == k)
            def _():
                t_pump(13 - 2 * k)
                t_pump(12 - 2 * k)

        @pl.when(i == 0)
        def _():
            z_last()

        @pl.when(i == 1)
        def _():
            z_pump(2, 0, (True, False))

        @pl.when(i == 2)
        def _():
            z_pump(2, 1, (False, True))

        @pl.when(i >= 3)
        def _():
            z_pump(hg, half, (True, True))

        @pl.when(i == 3)
        def _():
            for m in range(8):
                turned = jnp.transpose(lacc[rows(m * 128, 128), :])
                lrow[m // 2, m % 2 : m % 2 + 1, :] = jnp.sum(turned, axis=0, keepdims=True)
            for hg_, way, who, owner in l_peers():
                l_copy(hg_, way, who, owner).start()

    v_grad(6)
    for half in range(2):
        rs_copy(3, half, 0).start()

    loss = [lrow[3, 0:1, 64 * half : 64 * half + 32] for half in range(2)]
    for hg, way, who, owner in l_peers():
        l_copy(hg, way, who, owner).wait_recv()
        part = lrecv.at[(hg * 2 + way) * 2 + who]
        for half in range(2):
            if hg < 3:
                first = 64 * way + 32 * who
                loss[half] = loss[half] + part[half : half + 1, first : first + 32]
            else:
                first = 64 * half + 32 * who
                loss[half] = loss[half] + part[way : way + 1, first : first + 32]
    loss_ref[:, :32] = loss[0]
    loss_ref[:, 32:] = loss[1]

    for half in range(2):
        for part in range(2):
            own = text_row((OWN, half, part))
            total = t_sum((OWN, half, part))
            u = tf[rows(own, 16), :]
            first = 32 * half + 16 * part
            back = total - u * jnp.sum(u * total, axis=1, keepdims=True)
            tgrad_ref[rows(first, 16), :] = back * inv_t[rows(first, 16), :1]

    for half in range(2):
        own = 768 + 64 * half
        rs_copy(3, half, 0).wait_recv()
        total = vg[rows(own, 32), :] + recv_s[3, half, 0]
        for way in range(2):
            rz_copy(way, half, 0, own).wait_recv()
            total = total + recv_v[0, half, way]
        u = vf[rows(own, 32), :]
        back = total - u * jnp.sum(u * total, axis=1, keepdims=True)
        vgrad_ref[rows(32 * half, 32), :] = back * inv_v[rows(32 * half, 32), :1]

    def drain(ref, sem):
        pltpu.make_async_remote_copy(
            src_ref=ref, dst_ref=ref, send_sem=sem, recv_sem=sem, device_id=other, device_id_type=MESH
        ).wait_send()

    for way in range(4):
        drain(tf.at[rows(0, 240)], t_send.at[way])
        drain(tg.at[rows(0, 240)], rt_send.at[way])
    for way in range(2):
        drain(vf.at[rows(0, 224)], z_send.at[way])
        drain(vf.at[rows(0, 256)], s_send.at[way])
        drain(vg.at[rows(0, 224)], rz_send.at[way])
    drain(ids_all.at[0, pl.ds(0, 3)], i_send.at[0])
    drain(ids_all.at[pl.ds(0, 3)], i_send.at[1])
    drain(vg.at[rows(0, 512)], rs_send.at[0])
    drain(lrecv.at[pl.ds(0, 15)], l_send.at[0])


def hand_on(loss_ref, vgrad_ref, tgrad_ref, loss_out, vgrad_out, tgrad_out):
    loss_out[...] = loss_ref[...]
    vgrad_out[...] = vgrad_ref[...]
    tgrad_out[...] = tgrad_ref[...]


def shards(video, text, match_ids, log_scale, bias):
    vmem = pl.BlockSpec(memory_space=pltpu.VMEM)
    hbm = pl.BlockSpec(memory_space=pl.ANY)
    dma = pltpu.SemaphoreType.DMA
    loss, vgrad, tgrad = pl.pallas_call(
        kernel,
        out_shape=(
            jax.ShapeDtypeStruct((1, 64), F32),
            jax.ShapeDtypeStruct((64, 1024), F32),
            jax.ShapeDtypeStruct((64, 1024), F32),
        ),
        in_specs=[hbm] * 5,
        out_specs=(vmem, vmem, vmem),
        scratch_shapes=[
            pltpu.VMEM((1024, 1024), F32),
            pltpu.VMEM((1024, 1024), F32),
            pltpu.VMEM((1024, 1024), BF16),
            pltpu.VMEM((2, 1024, 1024), F8),
            pltpu.VMEM((1024, 1024), BF16),
            pltpu.VMEM((2, 1024, 1024), F8),
            pltpu.VMEM((256, 256), F32),
            pltpu.VMEM((8, 128, 1024), BF16),
            pltpu.VMEM((2, 8, 128, 1024), F8),
            pltpu.VMEM((1024, 1024), F32),
            pltpu.VMEM((1024, 1024), F32),
            pltpu.VMEM((1024, 1024), F32),
            pltpu.VMEM((4, 2, 2, 32, 1024), F32),
            pltpu.VMEM((4, 2, 2, 32, 1024), F32),
            pltpu.VMEM((4, 4, 4, 128), jnp.int32),
            pltpu.VMEM((4, 128), jnp.int32),
            pltpu.VMEM((8, 1, 128), jnp.int32),
            pltpu.VMEM((1024, 128), jnp.int32),
            pltpu.VMEM((1024, 128), F32),
            pltpu.VMEM((4, 2, 128), F32),
            pltpu.VMEM((16, 2, 128), F32),
            pltpu.VMEM((64, 128), F32),
            pltpu.VMEM((64, 128), F32),
            pltpu.VMEM((64, 1024), F32),
            pltpu.VMEM((64, 1024), F32),
            pltpu.SMEM((64,), jnp.int32),
            pltpu.SMEM((1,), F32),
            pltpu.SMEM((1,), F32),
            dma((4,)), dma((4, 15)),
            dma((2,)), dma((2, 14)),
            dma((2,)), dma((2, 16)),
            dma((2,)), dma((2, 4)),
            dma((4,)), dma((4, 15)),
            dma((2,)), dma((2, 2, 4)),
            dma((1,)), dma((4, 2, 2)),
            dma((1,)), dma((16,)), dma((5,)),
        ],
        compiler_params=pltpu.CompilerParams(
            collective_id=0, has_side_effects=True, vmem_limit_bytes=56 * 2**20
        ),
        cost_estimate=pl.CostEstimate(flops=18 * 2**30, bytes_accessed=2**20, transcendentals=3 * 2**20),
    )(video, text, match_ids, log_scale, bias)
    loss, vgrad, tgrad = pl.pallas_call(
        hand_on,
        out_shape=(
            jax.ShapeDtypeStruct((1, 64), F32),
            jax.ShapeDtypeStruct((64, 1024), F32),
            jax.ShapeDtypeStruct((64, 1024), F32),
        ),
        in_specs=[vmem] * 3,
        out_specs=(vmem,) * 3,
    )(loss, vgrad, tgrad)
    return loss.reshape(64), vgrad, tgrad


def solution(mesh):
    return jax.shard_map(
        shards,
        mesh=mesh,
        in_specs=(P(("row", "col"), None), P(("row", "col"), None), P(("row", "col")), P(), P()),
        out_specs=(P(("row", "col")), P(("row", "col"), None), P(("row", "col"), None)),
        check_vma=False,
    )
```

```python
import jax
import jax.numpy as jnp
from jax import lax
from jax.experimental import pallas as pl
from jax.experimental.pallas import tpu as pltpu
from jax.sharding import PartitionSpec as P

EPS = 1e-06
MESH = pl.DeviceIdType.MESH
F32 = jnp.float32
BF16 = jnp.bfloat16
F8 = jnp.float8_e4m3fn


OWN = -1


def make_source():
    source = {}
    for way in range(4):
        first, part = way // 2, way % 2
        across = (2, 3) if first == 0 else (0, 1)
        for k in range(2):
            source[way, k] = (OWN, first, k)
            source[way, 2 + k] = (OWN, 1 - first, k)
        source[way, 4] = (way, part)
        source[way, 5] = (across[0], 0)
        source[way, 6] = (across[1], 0)
        source[way, 7] = (across[0], 1)
        source[way, 8] = (across[1], 1)
        source[way, 9] = (way, 2 + part)
        source[way, 10] = (across[0], 4)
        source[way, 11] = (across[1], 4)
        source[way, 12] = (way, 7 if part else 5)
        source[way, 13] = (way, 8 if part else 6)
        source[way, 14] = (way, 11 if part else 10)
    return source


SOURCE = make_source()


def children(slot):
    return [key for key, value in sorted(SOURCE.items(), key=lambda item: item[0][1]) if value == slot]


def identity(slot):
    if slot[0] == OWN:
        return (0, 0, slot[1], slot[2])
    dx, dy, half, part = identity(SOURCE[slot])
    step = 1 if slot[0] % 2 else 3
    if slot[0] < 2:
        return ((dx + step) % 4, dy, half, part)
    return (dx, (dy + step) % 4, half, part)


def video_row(hg, half, way, who):
    if isinstance(hg, int) and hg == 3:
        return 896 * way + 64 * half + 32 * who
    return 128 + 256 * hg + 128 * half + 64 * way + 32 * who


def text_row(slot):
    if slot[0] == OWN:
        return 32 * slot[1] + 16 * slot[2]
    return 64 * (slot[1] + 1) + 16 * slot[0]


def dot_nn(a, b):
    return lax.dot_general(a, b, (((1,), (0,)), ((), ())), preferred_element_type=F32)


def dot_nt(a, b):
    return lax.dot_general(a, b, (((1,), (1,)), ((), ())), preferred_element_type=F32)


def dot_tn(a, b):
    return lax.dot_general(a, b, (((0,), (0,)), ((), ())), preferred_element_type=F32)


def split(x):
    hi = x.astype(BF16)
    return hi, x - hi.astype(F32)


HI8, LO8 = 2.0**8, 2.0**17
W_HI8, W_LO8 = 2.0**4, 2.0**13


def rows(start, size):
    if not isinstance(start, int):
        start = pl.multiple_of(start, size)
    return pl.ds(start, size)


def kernel(
    video_any, text_any, ids_any, log_scale_any, bias_any,
    loss_ref, vgrad_ref, tgrad_ref,
    vf, tf, vh, v8, th, t8, dots, w, w8, vg, tg, recv_t, recv_v, recv_s, ids_all, ids_own, ids_vec, vidx, lacc, lrow, lrecv, inv_v, inv_t, video_ref, text_ref, ids_ref, log_scale_ref, bias_ref,
    t_send, t_recv, z_send, z_recv, s_send, s_recv, i_send, i_recv,
    rt_send, rt_recv, rz_send, rz_recv, rs_send, rs_recv, l_send, l_recv, in_sem,
):
    row, col = lax.axis_index("row"), lax.axis_index("col")
    z, x, y, core = row // 4, row % 4, col // 2, col % 2

    def at(x_, y_, z_, core_):
        return (z_ * 4 + x_, y_ * 2 + core_)

    xp, xm, yp, ym = (x + 1) % 4, (x + 3) % 4, (y + 1) % 4, (y + 3) % 4
    t_out = (at(xp, y, z, core), at(xm, y, z, core), at(x, yp, z, core), at(x, ym, z, core))
    t_back = (t_out[1], t_out[0], t_out[3], t_out[2])
    line_x = tuple(at((x + d) % 4, y, z, core) for d in range(4))
    line_y = tuple(at(x, (y + d) % 4, z, core) for d in range(4))
    z_out = (at(x, y, (z + 1) % 8, core), at(x, y, (z + 7) % 8, core))
    z_back = (z_out[1], z_out[0])
    other = at(x, y, z, 1 - core)

    loads = [
        pltpu.make_async_copy(src, dst, in_sem.at[n])
        for n, (src, dst) in enumerate(
            (
                (text_any, text_ref), (video_any, video_ref), (ids_any, ids_ref),
                (log_scale_any, log_scale_ref), (bias_any, bias_ref),
            )
        )
    ]
    for load in loads:
        load.start()

    barrier = pltpu.get_barrier_semaphore()
    for peer in line_x[1:] + line_y[1:]:
        pl.semaphore_signal(barrier, inc=1, device_id=peer, device_id_type=MESH)
    pl.semaphore_signal(barrier, inc=1, device_id=other, device_id_type=MESH)
    for step in range(1, 8):
        for c in range(2):
            pl.semaphore_signal(barrier, inc=1, device_id=at(x, y, (z + step) % 8, c), device_id_type=MESH)

    def unit(ref, inv_ref):
        full = ref[...]
        inv = lax.rsqrt(jnp.sum(full * full, axis=1, keepdims=True) + EPS)
        inv_ref[...] = jnp.broadcast_to(inv, (64, 128))
        return full * inv

    loads[0].wait()
    tu = unit(text_ref, inv_t)
    tf[rows(0, 64), :] = tu
    loads[1].wait()
    vu = unit(video_ref, inv_v)
    for half in range(2):
        vf[rows(64 * half, 32), :] = vu[32 * half : 32 * half + 32]
    lane = lax.broadcasted_iota(jnp.int32, (1, 128), 1)
    loads[2].wait()
    for quarter in range(4):
        vec = jnp.zeros((1, 128), jnp.int32)
        for n in range(16):
            vec = jnp.where(lane % 16 == n, ids_ref[16 * quarter + n], vec)
        ids_own[quarter : quarter + 1, :] = vec

    def t_copy(slot):
        way, tick = slot
        return pltpu.make_async_remote_copy(
            src_ref=tf.at[rows(text_row(SOURCE[slot]), 16)], dst_ref=tf.at[rows(text_row(slot), 16)],
            send_sem=t_send.at[way], recv_sem=t_recv.at[way, tick],
            device_id=t_out[way], device_id_type=MESH,
        )

    def v_slot(tick, way):
        q = tick % 4
        return 128 + 256 * (tick // 4) + 128 * (q // 2) + 64 * way + 16 * (q % 2)

    def z_copy(way, tick, src, dst):
        return pltpu.make_async_remote_copy(
            src_ref=vf.at[rows(src, 16)], dst_ref=vf.at[rows(dst, 16)],
            send_sem=z_send.at[way], recv_sem=z_recv.at[way, tick],
            device_id=z_out[way], device_id_type=MESH,
        )

    def s_copy(way, tick, src):
        return pltpu.make_async_remote_copy(
            src_ref=vf.at[rows(src, 16)], dst_ref=vf.at[rows(src + 32, 16)],
            send_sem=s_send.at[way], recv_sem=s_recv.at[way, tick],
            device_id=other, device_id_type=MESH,
        )

    def ix_copy(d):
        return pltpu.make_async_remote_copy(
            src_ref=ids_own, dst_ref=ids_all.at[0, (4 - d) % 4],
            send_sem=i_send.at[0], recv_sem=i_recv.at[0, (4 - d) % 4],
            device_id=line_x[d], device_id_type=MESH,
        )

    def iy_copy(d):
        return pltpu.make_async_remote_copy(
            src_ref=ids_all.at[0], dst_ref=ids_all.at[(4 - d) % 4],
            send_sem=i_send.at[1], recv_sem=i_recv.at[1, (4 - d) % 4],
            device_id=line_y[d], device_id_type=MESH,
        )

    pl.semaphore_wait(barrier, 21)

    for d in range(1, 4):
        ix_copy(d).start()
    ids_all[0, 0] = ids_own[...]
    for part in range(2):
        for way in range(2):
            for q in (2 * part, 2 * part + 1):
                z_copy(way, q, 64 * (q // 2) + 16 * (q % 2), v_slot(q, way)).start()
        for way in range(4):
            t_copy((way, part)).start()
    for k in range(2, 4):
        for way in range(4):
            t_copy((way, k)).start()
    for q in range(4):
        s_copy(q // 2, 14 + q % 2, 64 * (q // 2) + 16 * (q % 2)).start()

    local = lax.broadcasted_iota(jnp.int32, (32, 128), 0)
    for hg in range(4):
        for half in range(2):
            for way in range(2):
                for who in range(2):
                    if hg < 3:
                        from_z = (z + (7 - hg if way == 0 else hg + 1)) % 8
                    else:
                        from_z = (z + 4 * way) % 8
                    from_core = core if who == 0 else 1 - core
                    base = ((from_z * 4 + x) * 8 + y * 2 + from_core) * 64 + 32 * half
                    vidx[rows(video_row(hg, half, way, who), 32), :] = local + base
    lacc[...] = jnp.zeros_like(lacc)

    loads[3].wait()
    loads[4].wait()
    scale = jnp.exp(jnp.full((1, 128), log_scale_ref[0], F32))
    bias = jnp.full((1, 128), bias_ref[0], F32)

    def t_split(start, size):
        full = tf[rows(start, size), :]
        hi, lo = split(full)
        th[rows(start, size), :] = hi
        t8[0, rows(start, size), :] = (lo * LO8).astype(F8)
        t8[1, rows(start, size), :] = (full * HI8).astype(F8)

    def v_split(start, size):
        full = vf[rows(start, size), :]
        hi, lo = split(full)
        vh[rows(start, size), :] = hi
        v8[0, rows(start, size), :] = (full * HI8).astype(F8)
        v8[1, rows(start, size), :] = (lo * LO8).astype(F8)

    def place(n):
        if isinstance(n, int):
            m = int(n**0.5)
            r = n - m * m
            return (r, m) if r <= m else (m, r - m - 1)
        m = (n >= 1).astype(jnp.int32) + (n >= 4).astype(jnp.int32) + (n >= 9).astype(jnp.int32)
        r = n - m * m
        return jnp.where(r <= m, r, m), jnp.where(r <= m, m, r - m - 1)

    def block_dots(n):
        vb, tb = place(n)
        vs, ts = rows(vb * 256, 256), rows(tb * 256, 256)
        small = dot_nt(
            jnp.concatenate([v8[0, vs, :], v8[1, vs, :]], axis=1), jnp.concatenate([t8[0, ts, :], t8[1, ts, :]], axis=1)
        )
        dots[...] = dot_nt(vh[vs, :], th[ts, :]) + small * (1.0 / (HI8 * LO8))

    def block_rest(n):
        vb, tb = place(n)
        vs = rows(vb * 256, 256)
        total = jnp.zeros((256, 128), F32)
        for half in range(2):
            logits = dots[:, 128 * half : 128 * half + 128] * scale + bias
            match = vidx[vs, :] == ids_vec[tb * 2 + half]
            q = jnp.where(match, -logits, logits)
            e = jnp.exp(q)
            u = 1.0 + e
            weight = (jnp.where(match, -scale, scale) * e) / u
            small = e * (1.0 - e * (0.5 - e * (1.0 / 3.0)))
            total = total + jnp.where(e < 1.0 / 64.0, small, jnp.log(u))
            hi, lo = split(weight)
            hi8, lo8 = (weight * W_HI8).astype(F8), (lo * W_LO8).astype(F8)
            cols = rows((tb * 2 + half) * 128, 128)
            for k in range(2):
                w[vb * 2 + k, :, cols] = hi[128 * k : 128 * k + 128]
                w8[0, vb * 2 + k, :, cols] = hi8[128 * k : 128 * k + 128]
                w8[1, vb * 2 + k, :, cols] = lo8[128 * k : 128 * k + 128]
        lacc[vs, :] += total

    def group_ids(group):
        vec = jnp.zeros((1, 128), jnp.int32)
        for spot in range(8):
            if spot >= 4:
                slot = (spot - 4, 2 * group)
            elif group > 0:
                slot = (spot, 2 * group - 1)
            else:
                slot = (OWN, spot // 2, spot % 2)
            dx, dy, half, part = identity(slot)
            ids = ids_all[dy, dx, pl.ds(2 * half + part, 1), :]
            vec = ids if spot == 0 else jnp.where(lane < 16 * spot, vec, ids)
        return vec

    def count(tick):
        done = 0
        for bound, more in ((2, 1), (6, 1), (7, 1), (8, 1), (10, 2), (11, 1), (12, 1), (13, 1), (14, 7)):
            done = done + jnp.where(tick >= bound, more, 0)
        return done

    @pl.loop(0, 15)
    def _(tick):
        for way in range(2):

            @pl.when(tick < 12)
            def _():
                slot = v_slot(tick, way)
                z_copy(way, tick, slot, slot).wait_recv()

                @pl.when(tick < 8)
                def _():
                    z_copy(way, tick + 4, slot, slot + 256).start()

                @pl.when((tick >= 8) & ((tick % 4) // 2 == way))
                def _():
                    last = 896 + 64 * way + 16 * (tick % 2)
                    z_copy(way, 12 + tick % 2, slot, last).start()

                s_copy(way, tick, slot).start()

            @pl.when((tick == 12) | (tick == 13))
            def _():
                slot = 896 + 64 * way + 16 * (tick % 2)
                z_copy(way, tick, slot, slot).wait_recv()
                s_copy(way, tick, slot).start()

            @pl.when((tick >= 1) & (tick <= 12))
            def _():
                s_copy(way, tick - 1, v_slot(tick - 1, way)).wait_recv()

            @pl.when(tick >= 13)
            def _():
                s_copy(way, tick - 1, 896 + 64 * way + 16 * ((tick - 1) % 2)).wait_recv()

            @pl.when(tick == 1)
            def _():
                for part in range(2):
                    s_copy(way, 14 + part, 64 * way + 16 * part).wait_recv()

        for k in range(15):

            @pl.when(tick == k)
            def _():
                for way in range(4):
                    t_copy((way, k)).wait_recv()
                    for child in children((way, k)):
                        t_copy(child).start()
                if k == 0:
                    for d in range(1, 4):
                        ix_copy(d).wait_recv()
                    for d in range(1, 4):
                        iy_copy(d).start()
                if k == 3:
                    for d in range(1, 4):
                        iy_copy(d).wait_recv()
                    for group in range(8):
                        ids_vec[group] = group_ids(group)

        @pl.when(tick % 2 == 0)
        def _():
            t_split(64 * tick, 128)

        @pl.when((tick == 1) | ((tick % 2 == 0) & (tick >= 2)))
        def _():
            v_split(jnp.where(tick == 1, 0, 64 * tick), 128)

        @pl.when(tick == 2)
        def _():
            block_dots(0)

        @pl.loop(jnp.maximum(count(tick - 1), 1), count(tick))
        def _(n):
            block_rest(n - 1)
            block_dots(n)

    block_rest(15)

    def rt_copy(slot):
        way, tick = slot
        row_ = text_row(slot)
        return pltpu.make_async_remote_copy(
            src_ref=tg.at[rows(row_, 16)], dst_ref=recv_t.at[rows(row_, 16)],
            send_sem=rt_send.at[way], recv_sem=rt_recv.at[way, tick],
            device_id=t_back[way], device_id_type=MESH,
        )

    def t_sum(slot):
        total = tg[rows(text_row(slot), 16), :]
        for child in children(slot):
            rt_copy(child).wait_recv()
            total = total + recv_t[rows(text_row(child), 16), :]
        return total

    def t_pump(tick):
        for way in range(4):
            slot = (way, tick)
            if children(slot):
                tg[rows(text_row(slot), 16), :] = t_sum(slot)
            rt_copy(slot).start()

    def rz_copy(way, half, step, src):
        return pltpu.make_async_remote_copy(
            src_ref=vg.at[rows(src, 32)], dst_ref=recv_v.at[step, half, way],
            send_sem=rz_send.at[way], recv_sem=rz_recv.at[way, half, step],
            device_id=z_back[way], device_id_type=MESH,
        )

    def rs_copy(hg, half, way):
        return pltpu.make_async_remote_copy(
            src_ref=vg.at[rows(video_row(hg, half, way, 1), 32)], dst_ref=recv_s.at[hg, half, way],
            send_sem=rs_send.at[0], recv_sem=rs_recv.at[hg, half, way],
            device_id=other, device_id_type=MESH,
        )

    def z_pump(hg, half, with_recv):
        for way in range(2):
            slot = video_row(hg, half, way, 0)
            rs_copy(hg, half, way).wait_recv()
            if with_recv[way]:
                rz_copy(way, half, hg + 1, slot).wait_recv()
                vg[rows(slot, 32), :] += recv_s[hg, half, way] + recv_v[hg + 1, half, way]
            else:
                vg[rows(slot, 32), :] += recv_s[hg, half, way]
            rz_copy(way, half, hg, slot).start()

    def z_last():
        for half in range(2):
            slot = 896 + 64 * half
            rs_copy(3, half, 1).wait_recv()
            vg[rows(slot, 32), :] += recv_s[3, half, 1]
            rz_copy(half, half, 3, slot).start()

    def t_grad(g):
        cols = pl.ds(pl.multiple_of(g * 128, 128), 128)
        hi = w[:, :, cols].reshape(1024, 128)
        lo8 = w8[1, :, :, cols].reshape(1024, 128)
        hi8 = w8[0, :, :, cols].reshape(1024, 128)
        small = dot_tn(jnp.concatenate([lo8, hi8], axis=0), v8[...].reshape(2048, 1024))
        tg[rows(g * 128, 128), :] = dot_tn(hi, vh[...]) + small * (1.0 / (W_HI8 * LO8))

    def v_grad(m):
        small = dot_nn(jnp.concatenate([w8[0, m], w8[1, m]], axis=1), t8[...].reshape(2048, 1024))
        vg[rows(m * 128, 128), :] = dot_nn(w[m], th[...]) + small * (1.0 / (W_HI8 * LO8))

    def l_copy(hg, way, who, owner):
        slot = (hg * 2 + way) * 2 + who
        return pltpu.make_async_remote_copy(
            src_ref=lrow.at[pl.ds(1 + 2 * hg if hg < 3 else 6 * way, 2)], dst_ref=lrecv.at[slot],
            send_sem=l_send.at[0], recv_sem=l_recv.at[slot],
            device_id=owner, device_id_type=MESH,
        )

    def l_peers():
        peers = []
        for hg in range(4):
            for way in range(2):
                if hg < 3:
                    to_z = (z + (7 - hg if way == 0 else hg + 1)) % 8
                else:
                    to_z = (z + 4 * way) % 8
                for who in range(2):
                    if (hg, way, who) != (3, 0, 0):
                        peers.append((hg, way, who, at(x, y, to_z, core if who == 0 else 1 - core)))
        return peers

    t_grad(7)
    t_pump(14)
    t_pump(13)

    @pl.loop(0, 7)
    def _(i):
        hg, half = 2 - (i - 1) // 2, (i - 1) % 2
        v_grad(jnp.where(i == 0, 7, 1 + 2 * hg + half))

        @pl.when(i == 0)
        def _():
            for half_ in range(2):
                rs_copy(3, half_, 1).start()

        @pl.when(i > 0)
        def _():
            for way in range(2):
                rs_copy(hg, half, way).start()

        t_grad(6 - i)
        @pl.when(i == 0)
        def _():
            z_last()

        @pl.when(i == 1)
        def _():
            z_pump(2, 0, (True, False))

        @pl.when(i == 2)
        def _():
            z_pump(2, 1, (False, True))

        @pl.when(i >= 3)
        def _():
            z_pump(hg, half, (True, True))

        for k in range(7):

            @pl.when(i == k)
            def _():
                t_pump(12 - 2 * k)
                if k < 6:
                    t_pump(11 - 2 * k)

        @pl.when(i == 3)
        def _():
            for m in range(8):
                turned = jnp.transpose(lacc[rows(m * 128, 128), :])
                lrow[m] = jnp.sum(turned, axis=0, keepdims=True)
            for hg_, way, who, owner in l_peers():
                l_copy(hg_, way, who, owner).start()

    v_grad(0)
    for half in range(2):
        rs_copy(3, half, 0).start()

    loss = [lrow[0, :, 64 * half : 64 * half + 32] for half in range(2)]
    for hg, way, who, owner in l_peers():
        l_copy(hg, way, who, owner).wait_recv()
        part = lrecv.at[(hg * 2 + way) * 2 + who]
        for half in range(2):
            if hg < 3:
                first = 64 * way + 32 * who
                loss[half] = loss[half] + part[half, :, first : first + 32]
            else:
                first = 64 * half + 32 * who
                loss[half] = loss[half] + part[way, :, first : first + 32]
    loss_ref[:, :32] = loss[0]
    loss_ref[:, 32:] = loss[1]

    for half in range(2):
        for part in range(2):
            own = text_row((OWN, half, part))
            total = t_sum((OWN, half, part))
            u = tf[rows(own, 16), :]
            first = 32 * half + 16 * part
            back = total - u * jnp.sum(u * total, axis=1, keepdims=True)
            tgrad_ref[rows(first, 16), :] = back * inv_t[rows(first, 16), :1]

    for half in range(2):
        own = 64 * half
        rs_copy(3, half, 0).wait_recv()
        total = vg[rows(own, 32), :] + recv_s[3, half, 0]
        for way in range(2):
            rz_copy(way, half, 0, own).wait_recv()
            total = total + recv_v[0, half, way]
        u = vf[rows(own, 32), :]
        back = total - u * jnp.sum(u * total, axis=1, keepdims=True)
        vgrad_ref[rows(32 * half, 32), :] = back * inv_v[rows(32 * half, 32), :1]

    def drain(ref, sem):
        pltpu.make_async_remote_copy(
            src_ref=ref, dst_ref=ref, send_sem=sem, recv_sem=sem, device_id=other, device_id_type=MESH
        ).wait_send()

    for way in range(4):
        drain(tf.at[rows(0, 240)], t_send.at[way])
        drain(tg.at[rows(0, 240)], rt_send.at[way])
    for way in range(2):
        drain(vf.at[rows(0, 224)], z_send.at[way])
        drain(vf.at[rows(0, 256)], s_send.at[way])
        drain(vg.at[rows(0, 224)], rz_send.at[way])
    drain(ids_all.at[0, pl.ds(0, 3)], i_send.at[0])
    drain(ids_all.at[pl.ds(0, 3)], i_send.at[1])
    drain(vg.at[rows(0, 512)], rs_send.at[0])
    drain(lrecv.at[pl.ds(0, 15)], l_send.at[0])


def hand_on(loss_ref, vgrad_ref, tgrad_ref, loss_out, vgrad_out, tgrad_out):
    loss_out[...] = loss_ref[...]
    vgrad_out[...] = vgrad_ref[...]
    tgrad_out[...] = tgrad_ref[...]


def shards(video, text, match_ids, log_scale, bias):
    vmem = pl.BlockSpec(memory_space=pltpu.VMEM)
    hbm = pl.BlockSpec(memory_space=pl.ANY)
    dma = pltpu.SemaphoreType.DMA
    loss, vgrad, tgrad = pl.pallas_call(
        kernel,
        out_shape=(
            jax.ShapeDtypeStruct((1, 64), F32),
            jax.ShapeDtypeStruct((64, 1024), F32),
            jax.ShapeDtypeStruct((64, 1024), F32),
        ),
        in_specs=[hbm] * 5,
        out_specs=(vmem, vmem, vmem),
        scratch_shapes=[
            pltpu.VMEM((1024, 1024), F32),
            pltpu.VMEM((1024, 1024), F32),
            pltpu.VMEM((1024, 1024), BF16),
            pltpu.VMEM((2, 1024, 1024), F8),
            pltpu.VMEM((1024, 1024), BF16),
            pltpu.VMEM((2, 1024, 1024), F8),
            pltpu.VMEM((256, 256), F32),
            pltpu.VMEM((8, 128, 1024), BF16),
            pltpu.VMEM((2, 8, 128, 1024), F8),
            pltpu.VMEM((1024, 1024), F32),
            pltpu.VMEM((1024, 1024), F32),
            pltpu.VMEM((1024, 1024), F32),
            pltpu.VMEM((4, 2, 2, 32, 1024), F32),
            pltpu.VMEM((4, 2, 2, 32, 1024), F32),
            pltpu.VMEM((4, 4, 4, 128), jnp.int32),
            pltpu.VMEM((4, 128), jnp.int32),
            pltpu.VMEM((8, 1, 128), jnp.int32),
            pltpu.VMEM((1024, 128), jnp.int32),
            pltpu.VMEM((1024, 128), F32),
            pltpu.VMEM((8, 1, 128), F32),
            pltpu.VMEM((16, 2, 1, 128), F32),
            pltpu.VMEM((64, 128), F32),
            pltpu.VMEM((64, 128), F32),
            pltpu.VMEM((64, 1024), F32),
            pltpu.VMEM((64, 1024), F32),
            pltpu.SMEM((64,), jnp.int32),
            pltpu.SMEM((1,), F32),
            pltpu.SMEM((1,), F32),
            dma((4,)), dma((4, 15)),
            dma((2,)), dma((2, 14)),
            dma((2,)), dma((2, 16)),
            dma((2,)), dma((2, 4)),
            dma((4,)), dma((4, 15)),
            dma((2,)), dma((2, 2, 4)),
            dma((1,)), dma((4, 2, 2)),
            dma((1,)), dma((16,)), dma((5,)),
        ],
        compiler_params=pltpu.CompilerParams(
            collective_id=0, has_side_effects=True, vmem_limit_bytes=56 * 2**20
        ),
        cost_estimate=pl.CostEstimate(flops=18 * 2**30, bytes_accessed=2**20, transcendentals=3 * 2**20),
    )(video, text, match_ids, log_scale, bias)
    loss, vgrad, tgrad = pl.pallas_call(
        hand_on,
        out_shape=(
            jax.ShapeDtypeStruct((1, 64), F32),
            jax.ShapeDtypeStruct((64, 1024), F32),
            jax.ShapeDtypeStruct((64, 1024), F32),
        ),
        in_specs=[vmem] * 3,
        out_specs=(vmem,) * 3,
    )(loss, vgrad, tgrad)
    return loss.reshape(64), vgrad, tgrad


def solution(mesh):
    return jax.shard_map(
        shards,
        mesh=mesh,
        in_specs=(P(("row", "col"), None), P(("row", "col"), None), P(("row", "col")), P(), P()),
        out_specs=(P(("row", "col")), P(("row", "col"), None), P(("row", "col"), None)),
        check_vma=False,
    )
```

```python
import jax
import jax.numpy as jnp
from jax import lax
from jax.experimental import pallas as pl
from jax.experimental.pallas import tpu as pltpu
from jax.sharding import PartitionSpec as P

EPS = 1e-06
MESH = pl.DeviceIdType.MESH
F32 = jnp.float32
BF16 = jnp.bfloat16
F8 = jnp.float8_e4m3fn


OWN = -1


def make_source():
    source = {}
    for way in range(4):
        first, part = way // 2, way % 2
        across = (2, 3) if first == 0 else (0, 1)
        for k in range(2):
            source[way, k] = (OWN, first, k)
            source[way, 2 + k] = (OWN, 1 - first, k)
        source[way, 4] = (way, part)
        source[way, 5] = (across[0], 0)
        source[way, 6] = (across[1], 0)
        source[way, 7] = (across[0], 1)
        source[way, 8] = (across[1], 1)
        source[way, 9] = (way, 2 + part)
        source[way, 10] = (across[0], 4)
        source[way, 11] = (across[1], 4)
        source[way, 12] = (way, 7 if part else 5)
        source[way, 13] = (way, 8 if part else 6)
        source[way, 14] = (way, 11 if part else 10)
    return source


SOURCE = make_source()


def children(slot):
    return [key for key, value in sorted(SOURCE.items(), key=lambda item: item[0][1]) if value == slot]


def identity(slot):
    if slot[0] == OWN:
        return (0, 0, slot[1], slot[2])
    dx, dy, half, part = identity(SOURCE[slot])
    step = 1 if slot[0] % 2 else 3
    if slot[0] < 2:
        return ((dx + step) % 4, dy, half, part)
    return (dx, (dy + step) % 4, half, part)


def video_row(hg, half, way, who):
    if isinstance(hg, int) and hg == 3:
        return 896 * way + 64 * half + 32 * who
    return 128 + 256 * hg + 128 * half + 64 * way + 32 * who


def text_row(slot):
    if slot[0] == OWN:
        return 32 * slot[1] + 16 * slot[2]
    return 64 * (slot[1] + 1) + 16 * slot[0]


def dot_nn(a, b):
    return lax.dot_general(a, b, (((1,), (0,)), ((), ())), preferred_element_type=F32)


def dot_nt(a, b):
    return lax.dot_general(a, b, (((1,), (1,)), ((), ())), preferred_element_type=F32)


def dot_tn(a, b):
    return lax.dot_general(a, b, (((0,), (0,)), ((), ())), preferred_element_type=F32)


def split(x):
    hi = x.astype(BF16)
    return hi, x - hi.astype(F32)


HI8, LO8 = 2.0**8, 2.0**17
W_HI8, W_LO8 = 2.0**4, 2.0**13


def rows(start, size):
    if not isinstance(start, int):
        start = pl.multiple_of(start, size)
    return pl.ds(start, size)


def kernel(
    video_any, text_any, ids_any, log_scale_any, bias_any,
    loss_ref, vgrad_ref, tgrad_ref,
    vf, tf, vh, v8, th, t8, dots, w, w8, vg, tg, recv_t, recv_v, recv_s, ids_all, ids_own, ids_vec, vidx, lacc, lrow, lrecv, inv_v, inv_t, video_ref, text_ref, ids_ref, log_scale_ref, bias_ref,
    t_send, t_recv, z_send, z_recv, s_send, s_recv, i_send, i_recv,
    rt_send, rt_recv, rz_send, rz_recv, rs_send, rs_recv, l_send, l_recv, in_sem,
):
    row, col = lax.axis_index("row"), lax.axis_index("col")
    z, x, y, core = row // 4, row % 4, col // 2, col % 2

    def at(x_, y_, z_, core_):
        return (z_ * 4 + x_, y_ * 2 + core_)

    xp, xm, yp, ym = (x + 1) % 4, (x + 3) % 4, (y + 1) % 4, (y + 3) % 4
    t_out = (at(xp, y, z, core), at(xm, y, z, core), at(x, yp, z, core), at(x, ym, z, core))
    t_back = (t_out[1], t_out[0], t_out[3], t_out[2])
    line_x = tuple(at((x + d) % 4, y, z, core) for d in range(4))
    line_y = tuple(at(x, (y + d) % 4, z, core) for d in range(4))
    z_out = (at(x, y, (z + 1) % 8, core), at(x, y, (z + 7) % 8, core))
    z_back = (z_out[1], z_out[0])
    other = at(x, y, z, 1 - core)

    loads = [
        pltpu.make_async_copy(src, dst, in_sem.at[n])
        for n, (src, dst) in enumerate(
            (
                (text_any, text_ref), (video_any, video_ref), (ids_any, ids_ref),
                (log_scale_any, log_scale_ref), (bias_any, bias_ref),
            )
        )
    ]
    for load in loads:
        load.start()

    barrier = pltpu.get_barrier_semaphore()
    for peer in line_x[1:] + line_y[1:]:
        pl.semaphore_signal(barrier, inc=1, device_id=peer, device_id_type=MESH)
    pl.semaphore_signal(barrier, inc=1, device_id=other, device_id_type=MESH)
    for peer in z_out:
        pl.semaphore_signal(barrier, inc=1, device_id=peer, device_id_type=MESH)

    def unit(ref, inv_ref):
        full = ref[...]
        inv = lax.rsqrt(jnp.sum(full * full, axis=1, keepdims=True) + EPS)
        inv_ref[...] = jnp.broadcast_to(inv, (64, 128))
        return full * inv

    loads[0].wait()
    tu = unit(text_ref, inv_t)
    tf[rows(0, 64), :] = tu
    loads[1].wait()
    vu = unit(video_ref, inv_v)
    for half in range(2):
        vf[rows(64 * half, 32), :] = vu[32 * half : 32 * half + 32]
    lane = lax.broadcasted_iota(jnp.int32, (1, 128), 1)
    loads[2].wait()
    for quarter in range(4):
        vec = jnp.zeros((1, 128), jnp.int32)
        for n in range(16):
            vec = jnp.where(lane % 16 == n, ids_ref[16 * quarter + n], vec)
        ids_own[quarter : quarter + 1, :] = vec

    def t_copy(slot):
        way, tick = slot
        return pltpu.make_async_remote_copy(
            src_ref=tf.at[rows(text_row(SOURCE[slot]), 16)], dst_ref=tf.at[rows(text_row(slot), 16)],
            send_sem=t_send.at[way], recv_sem=t_recv.at[way, tick],
            device_id=t_out[way], device_id_type=MESH,
        )

    def v_slot(tick, way):
        q = tick % 4
        return 128 + 256 * (tick // 4) + 128 * (q // 2) + 64 * way + 16 * (q % 2)

    def z_copy(way, tick, src, dst):
        return pltpu.make_async_remote_copy(
            src_ref=vf.at[rows(src, 16)], dst_ref=vf.at[rows(dst, 16)],
            send_sem=z_send.at[way], recv_sem=z_recv.at[way, tick],
            device_id=z_out[way], device_id_type=MESH,
        )

    def s_copy(way, tick, src):
        return pltpu.make_async_remote_copy(
            src_ref=vf.at[rows(src, 16)], dst_ref=vf.at[rows(src + 32, 16)],
            send_sem=s_send.at[way], recv_sem=s_recv.at[way, tick],
            device_id=other, device_id_type=MESH,
        )

    def ix_copy(d):
        return pltpu.make_async_remote_copy(
            src_ref=ids_own, dst_ref=ids_all.at[0, (4 - d) % 4],
            send_sem=i_send.at[0], recv_sem=i_recv.at[0, (4 - d) % 4],
            device_id=line_x[d], device_id_type=MESH,
        )

    def iy_copy(d):
        return pltpu.make_async_remote_copy(
            src_ref=ids_all.at[0], dst_ref=ids_all.at[(4 - d) % 4],
            send_sem=i_send.at[1], recv_sem=i_recv.at[1, (4 - d) % 4],
            device_id=line_y[d], device_id_type=MESH,
        )

    pl.semaphore_wait(barrier, 9)

    for d in range(1, 4):
        ix_copy(d).start()
    ids_all[0, 0] = ids_own[...]
    for part in range(2):
        for way in range(2):
            for q in (2 * part, 2 * part + 1):
                z_copy(way, q, 64 * (q // 2) + 16 * (q % 2), v_slot(q, way)).start()
        for way in range(4):
            t_copy((way, part)).start()
    for k in range(2, 4):
        for way in range(4):
            t_copy((way, k)).start()
    for q in range(4):
        s_copy(q // 2, 14 + q % 2, 64 * (q // 2) + 16 * (q % 2)).start()

    local = lax.broadcasted_iota(jnp.int32, (32, 128), 0)
    for hg in range(4):
        for half in range(2):
            for way in range(2):
                for who in range(2):
                    if hg < 3:
                        from_z = (z + (7 - hg if way == 0 else hg + 1)) % 8
                    else:
                        from_z = (z + 4 * way) % 8
                    from_core = core if who == 0 else 1 - core
                    base = ((from_z * 4 + x) * 8 + y * 2 + from_core) * 64 + 32 * half
                    vidx[rows(video_row(hg, half, way, who), 32), :] = local + base
    lacc[...] = jnp.zeros_like(lacc)

    loads[3].wait()
    loads[4].wait()
    scale = jnp.exp(jnp.full((1, 128), log_scale_ref[0], F32))
    bias = jnp.full((1, 128), bias_ref[0], F32)

    def t_split(start, size):
        full = tf[rows(start, size), :]
        hi, lo = split(full)
        th[rows(start, size), :] = hi
        t8[0, rows(start, size), :] = (lo * LO8).astype(F8)
        t8[1, rows(start, size), :] = (full * HI8).astype(F8)

    def v_split(start, size):
        full = vf[rows(start, size), :]
        hi, lo = split(full)
        vh[rows(start, size), :] = hi
        v8[0, rows(start, size), :] = (full * HI8).astype(F8)
        v8[1, rows(start, size), :] = (lo * LO8).astype(F8)

    def place(n):
        if isinstance(n, int):
            m = int(n**0.5)
            r = n - m * m
            return (r, m) if r <= m else (m, r - m - 1)
        m = (n >= 1).astype(jnp.int32) + (n >= 4).astype(jnp.int32) + (n >= 9).astype(jnp.int32)
        r = n - m * m
        return jnp.where(r <= m, r, m), jnp.where(r <= m, m, r - m - 1)

    def block_dots(n):
        vb, tb = place(n)
        vs, ts = rows(vb * 256, 256), rows(tb * 256, 256)
        small = dot_nt(
            jnp.concatenate([v8[0, vs, :], v8[1, vs, :]], axis=1), jnp.concatenate([t8[0, ts, :], t8[1, ts, :]], axis=1)
        )
        dots[...] = dot_nt(vh[vs, :], th[ts, :]) + small * (1.0 / (HI8 * LO8))

    def block_rest(n):
        vb, tb = place(n)
        vs = rows(vb * 256, 256)
        es = []
        for half in range(2):
            logits = dots[:, 128 * half : 128 * half + 128] * scale + bias
            match = vidx[vs, :] == ids_vec[tb * 2 + half]
            e = jnp.exp(jnp.where(match, -logits, logits))
            es.append(e)
            weight = (jnp.where(match, -scale, scale) * e) / (1.0 + e)
            hi, lo = split(weight)
            hi8, lo8 = (weight * W_HI8).astype(F8), (lo * W_LO8).astype(F8)
            cols = rows((tb * 2 + half) * 128, 128)
            for k in range(2):
                w[vb * 2 + k, :, cols] = hi[128 * k : 128 * k + 128]
                w8[0, vb * 2 + k, :, cols] = hi8[128 * k : 128 * k + 128]
                w8[1, vb * 2 + k, :, cols] = lo8[128 * k : 128 * k + 128]
        both = es[0] + es[1] + es[0] * es[1]
        small = both * (1.0 - both * (0.5 - both * (1.0 / 3.0)))
        lacc[vs, :] += jnp.where(both < 1.0 / 64.0, small, jnp.log(1.0 + both))

    def group_ids(group):
        vec = jnp.zeros((1, 128), jnp.int32)
        for spot in range(8):
            if spot >= 4:
                slot = (spot - 4, 2 * group)
            elif group > 0:
                slot = (spot, 2 * group - 1)
            else:
                slot = (OWN, spot // 2, spot % 2)
            dx, dy, half, part = identity(slot)
            ids = ids_all[dy, dx, pl.ds(2 * half + part, 1), :]
            vec = ids if spot == 0 else jnp.where(lane < 16 * spot, vec, ids)
        return vec

    def count(tick):
        done = 0
        for bound, more in ((2, 1), (6, 1), (7, 1), (8, 1), (10, 2), (11, 1), (12, 1), (13, 1), (14, 4)):
            done = done + jnp.where(tick >= bound, more, 0)
        return done

    @pl.loop(0, 15)
    def _(tick):
        for way in range(2):

            @pl.when(tick < 12)
            def _():
                slot = v_slot(tick, way)
                z_copy(way, tick, slot, slot).wait_recv()

                @pl.when(tick < 8)
                def _():
                    z_copy(way, tick + 4, slot, slot + 256).start()

                @pl.when((tick >= 8) & ((tick % 4) // 2 == way))
                def _():
                    last = 896 + 64 * way + 16 * (tick % 2)
                    z_copy(way, 12 + tick % 2, slot, last).start()

                s_copy(way, tick, slot).start()

            @pl.when((tick == 12) | (tick == 13))
            def _():
                slot = 896 + 64 * way + 16 * (tick % 2)
                z_copy(way, tick, slot, slot).wait_recv()
                s_copy(way, tick, slot).start()

            @pl.when((tick >= 1) & (tick <= 12))
            def _():
                s_copy(way, tick - 1, v_slot(tick - 1, way)).wait_recv()

            @pl.when(tick >= 13)
            def _():
                s_copy(way, tick - 1, 896 + 64 * way + 16 * ((tick - 1) % 2)).wait_recv()

            @pl.when(tick == 1)
            def _():
                for part in range(2):
                    s_copy(way, 14 + part, 64 * way + 16 * part).wait_recv()

        for k in range(15):

            @pl.when(tick == k)
            def _():
                for way in range(4):
                    t_copy((way, k)).wait_recv()
                    for child in children((way, k)):
                        t_copy(child).start()
                if k == 0:
                    for d in range(1, 4):
                        ix_copy(d).wait_recv()
                    for d in range(1, 4):
                        iy_copy(d).start()
                if k == 3:
                    for d in range(1, 4):
                        iy_copy(d).wait_recv()
                    for group in range(8):
                        ids_vec[group] = group_ids(group)

        @pl.when(tick % 2 == 0)
        def _():
            t_split(64 * tick, 128)

        @pl.when((tick == 1) | ((tick % 2 == 0) & (tick >= 2)))
        def _():
            v_split(jnp.where(tick == 1, 0, 64 * tick), 128)

        @pl.when(tick == 2)
        def _():
            block_dots(0)

        @pl.loop(jnp.maximum(count(tick - 1), 1), count(tick))
        def _(n):
            block_rest(n - 1)
            block_dots(n)

    block_rest(12)

    def rt_copy(slot):
        way, tick = slot
        row_ = text_row(slot)
        return pltpu.make_async_remote_copy(
            src_ref=tg.at[rows(row_, 16)], dst_ref=recv_t.at[rows(row_, 16)],
            send_sem=rt_send.at[way], recv_sem=rt_recv.at[way, tick],
            device_id=t_back[way], device_id_type=MESH,
        )

    def t_sum(slot):
        total = tg[rows(text_row(slot), 16), :]
        for child in children(slot):
            rt_copy(child).wait_recv()
            total = total + recv_t[rows(text_row(child), 16), :]
        return total

    def t_pump(tick):
        for way in range(4):
            slot = (way, tick)
            if children(slot):
                tg[rows(text_row(slot), 16), :] = t_sum(slot)
            rt_copy(slot).start()

    def rz_copy(way, half, step, src):
        return pltpu.make_async_remote_copy(
            src_ref=vg.at[rows(src, 32)], dst_ref=recv_v.at[step, half, way],
            send_sem=rz_send.at[way], recv_sem=rz_recv.at[way, half, step],
            device_id=z_back[way], device_id_type=MESH,
        )

    def rs_copy(hg, half, way):
        return pltpu.make_async_remote_copy(
            src_ref=vg.at[rows(video_row(hg, half, way, 1), 32)], dst_ref=recv_s.at[hg, half, way],
            send_sem=rs_send.at[0], recv_sem=rs_recv.at[hg, half, way],
            device_id=other, device_id_type=MESH,
        )

    def z_pump(hg, half, with_recv):
        for way in range(2):
            slot = video_row(hg, half, way, 0)
            rs_copy(hg, half, way).wait_recv()
            if with_recv[way]:
                rz_copy(way, half, hg + 1, slot).wait_recv()
                vg[rows(slot, 32), :] += recv_s[hg, half, way] + recv_v[hg + 1, half, way]
            else:
                vg[rows(slot, 32), :] += recv_s[hg, half, way]
            rz_copy(way, half, hg, slot).start()

    def z_last():
        for half in range(2):
            slot = 896 + 64 * half
            rs_copy(3, half, 1).wait_recv()
            vg[rows(slot, 32), :] += recv_s[3, half, 1]
            rz_copy(half, half, 3, slot).start()

    def t_grad(g):
        cols = pl.ds(pl.multiple_of(g * 128, 128), 128)
        hi = w[:, :, cols].reshape(1024, 128)
        lo8 = w8[1, :, :, cols].reshape(1024, 128)
        hi8 = w8[0, :, :, cols].reshape(1024, 128)
        small = dot_tn(jnp.concatenate([lo8, hi8], axis=0), v8[...].reshape(2048, 1024))
        tg[rows(g * 128, 128), :] = dot_tn(hi, vh[...]) + small * (1.0 / (W_HI8 * LO8))

    def v_grad(m):
        small = dot_nn(jnp.concatenate([w8[0, m], w8[1, m]], axis=1), t8[...].reshape(2048, 1024))
        vg[rows(m * 128, 128), :] = dot_nn(w[m], th[...]) + small * (1.0 / (W_HI8 * LO8))

    def l_copy(hg, way, who, owner):
        slot = (hg * 2 + way) * 2 + who
        return pltpu.make_async_remote_copy(
            src_ref=lrow.at[pl.ds(1 + 2 * hg if hg < 3 else 6 * way, 2)], dst_ref=lrecv.at[slot],
            send_sem=l_send.at[0], recv_sem=l_recv.at[slot],
            device_id=owner, device_id_type=MESH,
        )

    def l_peers():
        peers = []
        for hg in range(4):
            for way in range(2):
                if hg < 3:
                    to_z = (z + (7 - hg if way == 0 else hg + 1)) % 8
                else:
                    to_z = (z + 4 * way) % 8
                for who in range(2):
                    if (hg, way, who) != (3, 0, 0):
                        peers.append((hg, way, who, at(x, y, to_z, core if who == 0 else 1 - core)))
        return peers

    t_grad(7)
    t_pump(14)
    t_pump(13)

    @pl.loop(13, 16)
    def _(n):
        block_dots(n)
        block_rest(n)

    @pl.loop(0, 7)
    def _(i):
        hg, half = 2 - (i - 1) // 2, (i - 1) % 2
        v_grad(jnp.where(i == 0, 7, 1 + 2 * hg + half))

        @pl.when(i == 0)
        def _():
            for half_ in range(2):
                rs_copy(3, half_, 1).start()

        @pl.when(i > 0)
        def _():
            for way in range(2):
                rs_copy(hg, half, way).start()

        t_grad(6 - i)
        @pl.when(i == 0)
        def _():
            z_last()

        @pl.when(i == 1)
        def _():
            z_pump(2, 0, (True, False))

        @pl.when(i == 2)
        def _():
            z_pump(2, 1, (False, True))

        @pl.when(i >= 3)
        def _():
            z_pump(hg, half, (True, True))

        for k in range(7):

            @pl.when(i == k)
            def _():
                t_pump(12 - 2 * k)
                if k < 6:
                    t_pump(11 - 2 * k)

        @pl.when(i == 3)
        def _():
            for m in range(8):
                turned = jnp.transpose(lacc[rows(m * 128, 128), :])
                lrow[m] = jnp.sum(turned, axis=0, keepdims=True)
            for hg_, way, who, owner in l_peers():
                l_copy(hg_, way, who, owner).start()

    v_grad(0)
    for half in range(2):
        rs_copy(3, half, 0).start()

    loss = [lrow[0, :, 64 * half : 64 * half + 32] for half in range(2)]
    for hg, way, who, owner in l_peers():
        l_copy(hg, way, who, owner).wait_recv()
        part = lrecv.at[(hg * 2 + way) * 2 + who]
        for half in range(2):
            if hg < 3:
                first = 64 * way + 32 * who
                loss[half] = loss[half] + part[half, :, first : first + 32]
            else:
                first = 64 * half + 32 * who
                loss[half] = loss[half] + part[way, :, first : first + 32]
    loss_ref[:, :32] = loss[0]
    loss_ref[:, 32:] = loss[1]

    for half in range(2):
        for part in range(2):
            own = text_row((OWN, half, part))
            total = t_sum((OWN, half, part))
            u = tf[rows(own, 16), :]
            first = 32 * half + 16 * part
            back = total - u * jnp.sum(u * total, axis=1, keepdims=True)
            tgrad_ref[rows(first, 16), :] = back * inv_t[rows(first, 16), :1]

    for half in range(2):
        own = 64 * half
        rs_copy(3, half, 0).wait_recv()
        total = vg[rows(own, 32), :] + recv_s[3, half, 0]
        for way in range(2):
            rz_copy(way, half, 0, own).wait_recv()
            total = total + recv_v[0, half, way]
        u = vf[rows(own, 32), :]
        back = total - u * jnp.sum(u * total, axis=1, keepdims=True)
        vgrad_ref[rows(32 * half, 32), :] = back * inv_v[rows(32 * half, 32), :1]

    def drain(ref, sem):
        pltpu.make_async_remote_copy(
            src_ref=ref, dst_ref=ref, send_sem=sem, recv_sem=sem, device_id=other, device_id_type=MESH
        ).wait_send()

    for way in range(4):
        drain(tf.at[rows(0, 240)], t_send.at[way])
        drain(tg.at[rows(0, 240)], rt_send.at[way])
    for way in range(2):
        drain(vf.at[rows(0, 224)], z_send.at[way])
        drain(vf.at[rows(0, 256)], s_send.at[way])
        drain(vg.at[rows(0, 224)], rz_send.at[way])
    drain(ids_all.at[0, pl.ds(0, 3)], i_send.at[0])
    drain(ids_all.at[pl.ds(0, 3)], i_send.at[1])
    drain(vg.at[rows(0, 512)], rs_send.at[0])
    drain(lrecv.at[pl.ds(0, 15)], l_send.at[0])


def hand_on(loss_any, vgrad_any, tgrad_any, loss_out, vgrad_out, tgrad_out, loss, grads, sems):
    pieces = [(loss_any, loss, loss_out)]
    for n, (src, dst) in enumerate(((vgrad_any, vgrad_out), (tgrad_any, tgrad_out))):
        for part in range(2):
            here = pl.ds(32 * part, 32)
            pieces.append((src.at[here], grads.at[n, here], dst.at[here]))
    first = [pltpu.make_async_copy(a, b, sems.at[0, n]) for n, (a, b, _) in enumerate(pieces)]
    second = [pltpu.make_async_copy(b, c, sems.at[1, n]) for n, (_, b, c) in enumerate(pieces)]
    for copy in first:
        copy.start()
    for come, go in zip(first, second):
        come.wait()
        go.start()
    for copy in second:
        copy.wait()


def shards(video, text, match_ids, log_scale, bias):
    vmem = pl.BlockSpec(memory_space=pltpu.VMEM)
    hbm = pl.BlockSpec(memory_space=pl.ANY)
    dma = pltpu.SemaphoreType.DMA
    loss, vgrad, tgrad = pl.pallas_call(
        kernel,
        out_shape=(
            jax.ShapeDtypeStruct((1, 64), F32),
            jax.ShapeDtypeStruct((64, 1024), F32),
            jax.ShapeDtypeStruct((64, 1024), F32),
        ),
        in_specs=[hbm] * 5,
        out_specs=(vmem, vmem, vmem),
        scratch_shapes=[
            pltpu.VMEM((1024, 1024), F32),
            pltpu.VMEM((1024, 1024), F32),
            pltpu.VMEM((1024, 1024), BF16),
            pltpu.VMEM((2, 1024, 1024), F8),
            pltpu.VMEM((1024, 1024), BF16),
            pltpu.VMEM((2, 1024, 1024), F8),
            pltpu.VMEM((256, 256), F32),
            pltpu.VMEM((8, 128, 1024), BF16),
            pltpu.VMEM((2, 8, 128, 1024), F8),
            pltpu.VMEM((1024, 1024), F32),
            pltpu.VMEM((1024, 1024), F32),
            pltpu.VMEM((1024, 1024), F32),
            pltpu.VMEM((4, 2, 2, 32, 1024), F32),
            pltpu.VMEM((4, 2, 2, 32, 1024), F32),
            pltpu.VMEM((4, 4, 4, 128), jnp.int32),
            pltpu.VMEM((4, 128), jnp.int32),
            pltpu.VMEM((8, 1, 128), jnp.int32),
            pltpu.VMEM((1024, 128), jnp.int32),
            pltpu.VMEM((1024, 128), F32),
            pltpu.VMEM((8, 1, 128), F32),
            pltpu.VMEM((16, 2, 1, 128), F32),
            pltpu.VMEM((64, 128), F32),
            pltpu.VMEM((64, 128), F32),
            pltpu.VMEM((64, 1024), F32),
            pltpu.VMEM((64, 1024), F32),
            pltpu.SMEM((64,), jnp.int32),
            pltpu.SMEM((1,), F32),
            pltpu.SMEM((1,), F32),
            dma((4,)), dma((4, 15)),
            dma((2,)), dma((2, 14)),
            dma((2,)), dma((2, 16)),
            dma((2,)), dma((2, 4)),
            dma((4,)), dma((4, 15)),
            dma((2,)), dma((2, 2, 4)),
            dma((1,)), dma((4, 2, 2)),
            dma((1,)), dma((16,)), dma((5,)),
        ],
        compiler_params=pltpu.CompilerParams(
            collective_id=0, has_side_effects=True, vmem_limit_bytes=56 * 2**20
        ),
        cost_estimate=pl.CostEstimate(flops=18 * 2**30, bytes_accessed=2**20, transcendentals=3 * 2**20),
    )(video, text, match_ids, log_scale, bias)
    loss, vgrad, tgrad = pl.pallas_call(
        hand_on,
        out_shape=(
            jax.ShapeDtypeStruct((1, 64), F32),
            jax.ShapeDtypeStruct((64, 1024), F32),
            jax.ShapeDtypeStruct((64, 1024), F32),
        ),
        in_specs=[hbm] * 3,
        out_specs=(hbm,) * 3,
        scratch_shapes=[pltpu.VMEM((1, 64), F32), pltpu.VMEM((2, 64, 1024), F32), dma((2, 5))],
    )(loss, vgrad, tgrad)
    return loss.reshape(64), vgrad, tgrad


def solution(mesh):
    return jax.shard_map(
        shards,
        mesh=mesh,
        in_specs=(P(("row", "col"), None), P(("row", "col"), None), P(("row", "col")), P(), P()),
        out_specs=(P(("row", "col")), P(("row", "col"), None), P(("row", "col"), None)),
        check_vma=False,
    )
```

```python
import jax
import jax.numpy as jnp
from jax import lax
from jax.experimental import pallas as pl
from jax.experimental.pallas import tpu as pltpu
from jax.sharding import PartitionSpec as P

EPS = 1e-06
MESH = pl.DeviceIdType.MESH
F32 = jnp.float32
BF16 = jnp.bfloat16
F8 = jnp.float8_e4m3fn


OWN = -1


def make_source():
    source = {}
    for way in range(4):
        first, part = way // 2, way % 2
        across = (2, 3) if first == 0 else (0, 1)
        for k in range(2):
            source[way, k] = (OWN, first, k)
            source[way, 2 + k] = (OWN, 1 - first, k)
        source[way, 4] = (way, part)
        source[way, 5] = (across[0], 0)
        source[way, 6] = (across[1], 0)
        source[way, 7] = (across[0], 1)
        source[way, 8] = (across[1], 1)
        source[way, 9] = (way, 2 + part)
        source[way, 10] = (across[0], 4)
        source[way, 11] = (across[1], 4)
        source[way, 12] = (way, 7 if part else 5)
        source[way, 13] = (way, 8 if part else 6)
        source[way, 14] = (way, 11 if part else 10)
    return source


SOURCE = make_source()


def children(slot):
    return [key for key, value in sorted(SOURCE.items(), key=lambda item: item[0][1]) if value == slot]


def identity(slot):
    if slot[0] == OWN:
        return (0, 0, slot[1], slot[2])
    dx, dy, half, part = identity(SOURCE[slot])
    step = 1 if slot[0] % 2 else 3
    if slot[0] < 2:
        return ((dx + step) % 4, dy, half, part)
    return (dx, (dy + step) % 4, half, part)


def video_row(hg, half, way, who):
    if isinstance(hg, int) and hg == 3:
        return 896 * way + 64 * half + 32 * who
    return 128 + 256 * hg + 128 * half + 64 * way + 32 * who


def text_row(slot):
    if slot[0] == OWN:
        return 32 * slot[1] + 16 * slot[2]
    return 64 * (slot[1] + 1) + 16 * slot[0]


def dot_nn(a, b):
    return lax.dot_general(a, b, (((1,), (0,)), ((), ())), preferred_element_type=F32)


def dot_nt(a, b):
    return lax.dot_general(a, b, (((1,), (1,)), ((), ())), preferred_element_type=F32)


def dot_tn(a, b):
    return lax.dot_general(a, b, (((0,), (0,)), ((), ())), preferred_element_type=F32)


def split(x):
    hi = x.astype(BF16)
    return hi, x - hi.astype(F32)


HI8, LO8 = 2.0**8, 2.0**17
W_HI8, W_LO8 = 2.0**4, 2.0**13


def rows(start, size):
    if not isinstance(start, int):
        start = pl.multiple_of(start, size)
    return pl.ds(start, size)


def kernel(
    video_any, text_any, ids_any, log_scale_any, bias_any,
    loss_ref, vgrad_ref, tgrad_ref,
    vf, tf, vh, v8, th, t8, dots, w, w8, vg, tg, recv_t, recv_v, recv_s, ids_all, ids_own, ids_vec, vidx, lacc, lrow, lrecv, inv_v, inv_t, video_ref, text_ref, ids_ref, log_scale_ref, bias_ref,
    t_send, t_recv, z_send, z_recv, s_send, s_recv, i_send, i_recv,
    rt_send, rt_recv, rz_send, rz_recv, rs_send, rs_recv, l_send, l_recv, in_sem,
):
    row, col = lax.axis_index("row"), lax.axis_index("col")
    z, x, y, core = row // 4, row % 4, col // 2, col % 2

    def at(x_, y_, z_, core_):
        return (z_ * 4 + x_, y_ * 2 + core_)

    xp, xm, yp, ym = (x + 1) % 4, (x + 3) % 4, (y + 1) % 4, (y + 3) % 4
    t_out = (at(xp, y, z, core), at(xm, y, z, core), at(x, yp, z, core), at(x, ym, z, core))
    t_back = (t_out[1], t_out[0], t_out[3], t_out[2])
    line_x = tuple(at((x + d) % 4, y, z, core) for d in range(4))
    line_y = tuple(at(x, (y + d) % 4, z, core) for d in range(4))
    z_out = (at(x, y, (z + 1) % 8, core), at(x, y, (z + 7) % 8, core))
    z_back = (z_out[1], z_out[0])
    other = at(x, y, z, 1 - core)

    loads = [
        pltpu.make_async_copy(src, dst, in_sem.at[n])
        for n, (src, dst) in enumerate(
            (
                (text_any, text_ref), (video_any, video_ref), (ids_any, ids_ref),
                (log_scale_any, log_scale_ref), (bias_any, bias_ref),
            )
        )
    ]
    for load in loads:
        load.start()

    barrier = pltpu.get_barrier_semaphore()
    for peer in line_x[1:] + line_y[1:]:
        pl.semaphore_signal(barrier, inc=1, device_id=peer, device_id_type=MESH)
    pl.semaphore_signal(barrier, inc=1, device_id=other, device_id_type=MESH)
    for peer in z_out:
        pl.semaphore_signal(barrier, inc=1, device_id=peer, device_id_type=MESH)

    def unit(ref, inv_ref):
        full = ref[...]
        inv = lax.rsqrt(jnp.sum(full * full, axis=1, keepdims=True) + EPS)
        inv_ref[...] = jnp.broadcast_to(inv, (64, 128))
        return full * inv

    loads[0].wait()
    tu = unit(text_ref, inv_t)
    tf[rows(0, 64), :] = tu
    loads[1].wait()
    vu = unit(video_ref, inv_v)
    for half in range(2):
        vf[rows(64 * half, 32), :] = vu[32 * half : 32 * half + 32]
    lane = lax.broadcasted_iota(jnp.int32, (1, 128), 1)
    loads[2].wait()
    for quarter in range(4):
        vec = jnp.zeros((1, 128), jnp.int32)
        for n in range(16):
            vec = jnp.where(lane % 16 == n, ids_ref[16 * quarter + n], vec)
        ids_own[quarter : quarter + 1, :] = vec

    def t_copy(slot):
        way, tick = slot
        return pltpu.make_async_remote_copy(
            src_ref=tf.at[rows(text_row(SOURCE[slot]), 16)], dst_ref=tf.at[rows(text_row(slot), 16)],
            send_sem=t_send.at[way], recv_sem=t_recv.at[way, tick],
            device_id=t_out[way], device_id_type=MESH,
        )

    def v_slot(tick, way):
        q = tick % 4
        return 128 + 256 * (tick // 4) + 128 * (q // 2) + 64 * way + 16 * (q % 2)

    def z_copy(way, tick, src, dst):
        return pltpu.make_async_remote_copy(
            src_ref=vf.at[rows(src, 16)], dst_ref=vf.at[rows(dst, 16)],
            send_sem=z_send.at[way], recv_sem=z_recv.at[way, tick],
            device_id=z_out[way], device_id_type=MESH,
        )

    def s_copy(way, tick, src):
        return pltpu.make_async_remote_copy(
            src_ref=vf.at[rows(src, 16)], dst_ref=vf.at[rows(src + 32, 16)],
            send_sem=s_send.at[way], recv_sem=s_recv.at[way, tick],
            device_id=other, device_id_type=MESH,
        )

    def ix_copy(d):
        return pltpu.make_async_remote_copy(
            src_ref=ids_own, dst_ref=ids_all.at[0, (4 - d) % 4],
            send_sem=i_send.at[0], recv_sem=i_recv.at[0, (4 - d) % 4],
            device_id=line_x[d], device_id_type=MESH,
        )

    def iy_copy(d):
        return pltpu.make_async_remote_copy(
            src_ref=ids_all.at[0], dst_ref=ids_all.at[(4 - d) % 4],
            send_sem=i_send.at[1], recv_sem=i_recv.at[1, (4 - d) % 4],
            device_id=line_y[d], device_id_type=MESH,
        )

    pl.semaphore_wait(barrier, 9)

    for d in range(1, 4):
        ix_copy(d).start()
    ids_all[0, 0] = ids_own[...]
    for part in range(2):
        for way in range(2):
            for q in (2 * part, 2 * part + 1):
                z_copy(way, q, 64 * (q // 2) + 16 * (q % 2), v_slot(q, way)).start()
        for way in range(4):
            t_copy((way, part)).start()
    for k in range(2, 4):
        for way in range(4):
            t_copy((way, k)).start()
    for q in range(4):
        s_copy(q // 2, 14 + q % 2, 64 * (q // 2) + 16 * (q % 2)).start()

    local = lax.broadcasted_iota(jnp.int32, (32, 128), 0)
    for hg in range(4):
        for half in range(2):
            for way in range(2):
                for who in range(2):
                    if hg < 3:
                        from_z = (z + (7 - hg if way == 0 else hg + 1)) % 8
                    else:
                        from_z = (z + 4 * way) % 8
                    from_core = core if who == 0 else 1 - core
                    base = ((from_z * 4 + x) * 8 + y * 2 + from_core) * 64 + 32 * half
                    vidx[rows(video_row(hg, half, way, who), 32), :] = local + base
    lacc[...] = jnp.zeros_like(lacc)

    loads[3].wait()
    loads[4].wait()
    scale = jnp.exp(jnp.full((1, 128), log_scale_ref[0], F32))
    bias = jnp.full((1, 128), bias_ref[0], F32)

    def t_split(start, size):
        full = tf[rows(start, size), :]
        hi, lo = split(full)
        th[rows(start, size), :] = hi
        t8[0, rows(start, size), :] = (lo * LO8).astype(F8)
        t8[1, rows(start, size), :] = (full * HI8).astype(F8)

    def v_split(start, size):
        full = vf[rows(start, size), :]
        hi, lo = split(full)
        vh[rows(start, size), :] = hi
        v8[0, rows(start, size), :] = (full * HI8).astype(F8)
        v8[1, rows(start, size), :] = (lo * LO8).astype(F8)

    def place(n):
        if isinstance(n, int):
            m = int(n**0.5)
            r = n - m * m
            return (r, m) if r <= m else (m, r - m - 1)
        m = (n >= 1).astype(jnp.int32) + (n >= 4).astype(jnp.int32) + (n >= 9).astype(jnp.int32)
        r = n - m * m
        return jnp.where(r <= m, r, m), jnp.where(r <= m, m, r - m - 1)

    def some_dots(start, size, tb):
        vs, ts = rows(start, size), rows(tb * 256, 256)
        small = dot_nt(
            jnp.concatenate([v8[0, vs, :], v8[1, vs, :]], axis=1), jnp.concatenate([t8[0, ts, :], t8[1, ts, :]], axis=1)
        )
        dots[:size, :] = dot_nt(vh[vs, :], th[ts, :]) + small * (1.0 / (HI8 * LO8))

    def some_rest(start, size, tb):
        vs = rows(start, size)
        es = []
        for half in range(2):
            logits = dots[:size, 128 * half : 128 * half + 128] * scale + bias
            match = vidx[vs, :] == ids_vec[tb * 2 + half]
            e = jnp.exp(jnp.where(match, -logits, logits))
            es.append(e)
            weight = (jnp.where(match, -scale, scale) * e) / (1.0 + e)
            hi, lo = split(weight)
            hi8, lo8 = (weight * W_HI8).astype(F8), (lo * W_LO8).astype(F8)
            cols = rows((tb * 2 + half) * 128, 128)
            for k in range(size // 128):
                w[start // 128 + k, :, cols] = hi[128 * k : 128 * k + 128]
                w8[0, start // 128 + k, :, cols] = hi8[128 * k : 128 * k + 128]
                w8[1, start // 128 + k, :, cols] = lo8[128 * k : 128 * k + 128]
        both = es[0] + es[1] + es[0] * es[1]
        small = both * (1.0 - both * (0.5 - both * (1.0 / 3.0)))
        lacc[vs, :] += jnp.where(both < 1.0 / 64.0, small, jnp.log(1.0 + both))

    def block_dots(n):
        vb, tb = place(n)
        some_dots(vb * 256, 256, tb)

    def block_rest(n):
        vb, tb = place(n)
        some_rest(vb * 256, 256, tb)

    def group_ids(group):
        vec = jnp.zeros((1, 128), jnp.int32)
        for spot in range(8):
            if spot >= 4:
                slot = (spot - 4, 2 * group)
            elif group > 0:
                slot = (spot, 2 * group - 1)
            else:
                slot = (OWN, spot // 2, spot % 2)
            dx, dy, half, part = identity(slot)
            ids = ids_all[dy, dx, pl.ds(2 * half + part, 1), :]
            vec = ids if spot == 0 else jnp.where(lane < 16 * spot, vec, ids)
        return vec

    def count(tick):
        done = 0
        for bound, more in ((2, 1), (6, 1), (7, 1), (8, 1), (10, 2), (11, 1), (12, 1), (13, 1)):
            done = done + jnp.where(tick >= bound, more, 0)
        return done

    @pl.loop(0, 15)
    def _(tick):
        for way in range(2):

            @pl.when(tick < 12)
            def _():
                slot = v_slot(tick, way)
                z_copy(way, tick, slot, slot).wait_recv()

                @pl.when(tick < 8)
                def _():
                    z_copy(way, tick + 4, slot, slot + 256).start()

                @pl.when((tick >= 8) & ((tick % 4) // 2 == way))
                def _():
                    last = 896 + 64 * way + 16 * (tick % 2)
                    z_copy(way, 12 + tick % 2, slot, last).start()

                s_copy(way, tick, slot).start()

            @pl.when((tick == 12) | (tick == 13))
            def _():
                slot = 896 + 64 * way + 16 * (tick % 2)
                z_copy(way, tick, slot, slot).wait_recv()
                s_copy(way, tick, slot).start()

            @pl.when((tick >= 1) & (tick <= 12))
            def _():
                s_copy(way, tick - 1, v_slot(tick - 1, way)).wait_recv()

            @pl.when(tick >= 13)
            def _():
                s_copy(way, tick - 1, 896 + 64 * way + 16 * ((tick - 1) % 2)).wait_recv()

            @pl.when(tick == 1)
            def _():
                for part in range(2):
                    s_copy(way, 14 + part, 64 * way + 16 * part).wait_recv()

        for k in range(15):

            @pl.when(tick == k)
            def _():
                for way in range(4):
                    t_copy((way, k)).wait_recv()
                    for child in children((way, k)):
                        t_copy(child).start()
                if k == 0:
                    for d in range(1, 4):
                        ix_copy(d).wait_recv()
                    for d in range(1, 4):
                        iy_copy(d).start()
                if k == 3:
                    for d in range(1, 4):
                        iy_copy(d).wait_recv()
                    for group in range(8):
                        ids_vec[group] = group_ids(group)

        @pl.when(tick % 2 == 0)
        def _():
            t_split(64 * tick, 128)

        @pl.when((tick == 1) | ((tick % 2 == 0) & (tick >= 2)))
        def _():
            v_split(jnp.where(tick == 1, 0, 64 * tick), 128)

        @pl.when(tick == 2)
        def _():
            block_dots(0)

        @pl.loop(jnp.maximum(count(tick - 1), 1), count(tick))
        def _(n):
            block_rest(n - 1)
            block_dots(n)

    block_rest(8)

    @pl.loop(0, 1)
    def _(n):
        some_dots(n * 1024, 1024, 3)
        some_rest(n * 1024, 1024, 3)

    def rt_copy(slot):
        way, tick = slot
        row_ = text_row(slot)
        return pltpu.make_async_remote_copy(
            src_ref=tg.at[rows(row_, 16)], dst_ref=recv_t.at[rows(row_, 16)],
            send_sem=rt_send.at[way], recv_sem=rt_recv.at[way, tick],
            device_id=t_back[way], device_id_type=MESH,
        )

    def t_sum(slot):
        total = tg[rows(text_row(slot), 16), :]
        for child in children(slot):
            rt_copy(child).wait_recv()
            total = total + recv_t[rows(text_row(child), 16), :]
        return total

    def t_pump(tick):
        for way in range(4):
            slot = (way, tick)
            if children(slot):
                tg[rows(text_row(slot), 16), :] = t_sum(slot)
            rt_copy(slot).start()

    def rz_copy(way, half, step, src):
        return pltpu.make_async_remote_copy(
            src_ref=vg.at[rows(src, 32)], dst_ref=recv_v.at[step, half, way],
            send_sem=rz_send.at[way], recv_sem=rz_recv.at[way, half, step],
            device_id=z_back[way], device_id_type=MESH,
        )

    def rs_copy(hg, half, way):
        return pltpu.make_async_remote_copy(
            src_ref=vg.at[rows(video_row(hg, half, way, 1), 32)], dst_ref=recv_s.at[hg, half, way],
            send_sem=rs_send.at[0], recv_sem=rs_recv.at[hg, half, way],
            device_id=other, device_id_type=MESH,
        )

    def z_pump(hg, half, with_recv):
        for way in range(2):
            slot = video_row(hg, half, way, 0)
            rs_copy(hg, half, way).wait_recv()
            if with_recv[way]:
                rz_copy(way, half, hg + 1, slot).wait_recv()
                vg[rows(slot, 32), :] += recv_s[hg, half, way] + recv_v[hg + 1, half, way]
            else:
                vg[rows(slot, 32), :] += recv_s[hg, half, way]
            rz_copy(way, half, hg, slot).start()

    def z_last():
        for half in range(2):
            slot = 896 + 64 * half
            rs_copy(3, half, 1).wait_recv()
            vg[rows(slot, 32), :] += recv_s[3, half, 1]
            rz_copy(half, half, 3, slot).start()

    def t_grad(g):
        cols = pl.ds(pl.multiple_of(g * 128, 128), 128)
        hi = w[:, :, cols].reshape(1024, 128)
        lo8 = w8[1, :, :, cols].reshape(1024, 128)
        hi8 = w8[0, :, :, cols].reshape(1024, 128)
        small = dot_tn(jnp.concatenate([lo8, hi8], axis=0), v8[...].reshape(2048, 1024))
        tg[rows(g * 128, 128), :] = dot_tn(hi, vh[...]) + small * (1.0 / (W_HI8 * LO8))

    def v_grad(m):
        small = dot_nn(jnp.concatenate([w8[0, m], w8[1, m]], axis=1), t8[...].reshape(2048, 1024))
        vg[rows(m * 128, 128), :] = dot_nn(w[m], th[...]) + small * (1.0 / (W_HI8 * LO8))

    def l_copy(hg, way, who, owner):
        slot = (hg * 2 + way) * 2 + who
        return pltpu.make_async_remote_copy(
            src_ref=lrow.at[pl.ds(1 + 2 * hg if hg < 3 else 6 * way, 2)], dst_ref=lrecv.at[slot],
            send_sem=l_send.at[0], recv_sem=l_recv.at[slot],
            device_id=owner, device_id_type=MESH,
        )

    def l_peers():
        peers = []
        for hg in range(4):
            for way in range(2):
                if hg < 3:
                    to_z = (z + (7 - hg if way == 0 else hg + 1)) % 8
                else:
                    to_z = (z + 4 * way) % 8
                for who in range(2):
                    if (hg, way, who) != (3, 0, 0):
                        peers.append((hg, way, who, at(x, y, to_z, core if who == 0 else 1 - core)))
        return peers

    t_grad(7)
    t_pump(14)
    t_pump(13)

    @pl.loop(13, 16)
    def _(n):
        block_dots(n)
        block_rest(n)

    @pl.loop(0, 7)
    def _(i):
        hg, half = 2 - (i - 1) // 2, (i - 1) % 2
        v_grad(jnp.where(i == 0, 7, 1 + 2 * hg + half))

        @pl.when(i == 0)
        def _():
            for half_ in range(2):
                rs_copy(3, half_, 1).start()

        @pl.when(i > 0)
        def _():
            for way in range(2):
                rs_copy(hg, half, way).start()

        t_grad(6 - i)
        @pl.when(i == 0)
        def _():
            z_last()

        @pl.when(i == 1)
        def _():
            z_pump(2, 0, (True, False))

        @pl.when(i == 2)
        def _():
            z_pump(2, 1, (False, True))

        @pl.when(i >= 3)
        def _():
            z_pump(hg, half, (True, True))

        for k in range(7):

            @pl.when(i == k)
            def _():
                t_pump(12 - 2 * k)
                if k < 6:
                    t_pump(11 - 2 * k)

        @pl.when(i == 3)
        def _():
            ones = jnp.ones((16, 128), BF16)
            hi, lo = split(lacc[...])
            sums = dot_nt(ones, hi) + dot_nt(ones, lo.astype(BF16))
            for m in range(8):
                lrow[m] = sums[:1, 128 * m : 128 * m + 128]
            for hg_, way, who, owner in l_peers():
                l_copy(hg_, way, who, owner).start()

    v_grad(0)
    for half in range(2):
        rs_copy(3, half, 0).start()

    loss = [lrow[0, :, 64 * half : 64 * half + 32] for half in range(2)]
    for hg, way, who, owner in l_peers():
        l_copy(hg, way, who, owner).wait_recv()
        part = lrecv.at[(hg * 2 + way) * 2 + who]
        for half in range(2):
            if hg < 3:
                first = 64 * way + 32 * who
                loss[half] = loss[half] + part[half, :, first : first + 32]
            else:
                first = 64 * half + 32 * who
                loss[half] = loss[half] + part[way, :, first : first + 32]
    loss_ref[:, :32] = loss[0]
    loss_ref[:, 32:] = loss[1]

    for half in range(2):
        for part in range(2):
            own = text_row((OWN, half, part))
            total = t_sum((OWN, half, part))
            u = tf[rows(own, 16), :]
            first = 32 * half + 16 * part
            back = total - u * jnp.sum(u * total, axis=1, keepdims=True)
            tgrad_ref[rows(first, 16), :] = back * inv_t[rows(first, 16), :1]

    for half in range(2):
        own = 64 * half
        rs_copy(3, half, 0).wait_recv()
        total = vg[rows(own, 32), :] + recv_s[3, half, 0]
        for way in range(2):
            rz_copy(way, half, 0, own).wait_recv()
            total = total + recv_v[0, half, way]
        u = vf[rows(own, 32), :]
        back = total - u * jnp.sum(u * total, axis=1, keepdims=True)
        vgrad_ref[rows(32 * half, 32), :] = back * inv_v[rows(32 * half, 32), :1]

    def drain(ref, sem):
        pltpu.make_async_remote_copy(
            src_ref=ref, dst_ref=ref, send_sem=sem, recv_sem=sem, device_id=other, device_id_type=MESH
        ).wait_send()

    for way in range(4):
        drain(tf.at[rows(0, 240)], t_send.at[way])
        drain(tg.at[rows(0, 240)], rt_send.at[way])
    for way in range(2):
        drain(vf.at[rows(0, 224)], z_send.at[way])
        drain(vf.at[rows(0, 256)], s_send.at[way])
        drain(vg.at[rows(0, 224)], rz_send.at[way])
    drain(ids_all.at[0, pl.ds(0, 3)], i_send.at[0])
    drain(ids_all.at[pl.ds(0, 3)], i_send.at[1])
    drain(vg.at[rows(0, 512)], rs_send.at[0])
    drain(lrecv.at[pl.ds(0, 15)], l_send.at[0])


def hand_on(loss_any, vgrad_any, tgrad_any, loss_out, vgrad_out, tgrad_out, loss, grads, sems):
    pieces = [(loss_any, loss, loss_out)]
    for n, (src, dst) in enumerate(((vgrad_any, vgrad_out), (tgrad_any, tgrad_out))):
        for part in range(2):
            here = pl.ds(32 * part, 32)
            pieces.append((src.at[here], grads.at[n, here], dst.at[here]))
    first = [pltpu.make_async_copy(a, b, sems.at[0, n]) for n, (a, b, _) in enumerate(pieces)]
    second = [pltpu.make_async_copy(b, c, sems.at[1, n]) for n, (_, b, c) in enumerate(pieces)]
    for copy in first:
        copy.start()
    for come, go in zip(first, second):
        come.wait()
        go.start()
    for copy in second:
        copy.wait()


def shards(video, text, match_ids, log_scale, bias):
    vmem = pl.BlockSpec(memory_space=pltpu.VMEM)
    hbm = pl.BlockSpec(memory_space=pl.ANY)
    dma = pltpu.SemaphoreType.DMA
    loss, vgrad, tgrad = pl.pallas_call(
        kernel,
        out_shape=(
            jax.ShapeDtypeStruct((1, 64), F32),
            jax.ShapeDtypeStruct((64, 1024), F32),
            jax.ShapeDtypeStruct((64, 1024), F32),
        ),
        in_specs=[hbm] * 5,
        out_specs=(vmem, vmem, vmem),
        scratch_shapes=[
            pltpu.VMEM((1024, 1024), F32),
            pltpu.VMEM((1024, 1024), F32),
            pltpu.VMEM((1024, 1024), BF16),
            pltpu.VMEM((2, 1024, 1024), F8),
            pltpu.VMEM((1024, 1024), BF16),
            pltpu.VMEM((2, 1024, 1024), F8),
            pltpu.VMEM((1024, 256), F32),
            pltpu.VMEM((8, 128, 1024), BF16),
            pltpu.VMEM((2, 8, 128, 1024), F8),
            pltpu.VMEM((1024, 1024), F32),
            pltpu.VMEM((1024, 1024), F32),
            pltpu.VMEM((1024, 1024), F32),
            pltpu.VMEM((4, 2, 2, 32, 1024), F32),
            pltpu.VMEM((4, 2, 2, 32, 1024), F32),
            pltpu.VMEM((4, 4, 4, 128), jnp.int32),
            pltpu.VMEM((4, 128), jnp.int32),
            pltpu.VMEM((8, 1, 128), jnp.int32),
            pltpu.VMEM((1024, 128), jnp.int32),
            pltpu.VMEM((1024, 128), F32),
            pltpu.VMEM((8, 1, 128), F32),
            pltpu.VMEM((16, 2, 1, 128), F32),
            pltpu.VMEM((64, 128), F32),
            pltpu.VMEM((64, 128), F32),
            pltpu.VMEM((64, 1024), F32),
            pltpu.VMEM((64, 1024), F32),
            pltpu.SMEM((64,), jnp.int32),
            pltpu.SMEM((1,), F32),
            pltpu.SMEM((1,), F32),
            dma((4,)), dma((4, 15)),
            dma((2,)), dma((2, 14)),
            dma((2,)), dma((2, 16)),
            dma((2,)), dma((2, 4)),
            dma((4,)), dma((4, 15)),
            dma((2,)), dma((2, 2, 4)),
            dma((1,)), dma((4, 2, 2)),
            dma((1,)), dma((16,)), dma((5,)),
        ],
        compiler_params=pltpu.CompilerParams(
            collective_id=0, has_side_effects=True, vmem_limit_bytes=56 * 2**20
        ),
        cost_estimate=pl.CostEstimate(flops=18 * 2**30, bytes_accessed=2**20, transcendentals=3 * 2**20),
    )(video, text, match_ids, log_scale, bias)
    loss, vgrad, tgrad = pl.pallas_call(
        hand_on,
        out_shape=(
            jax.ShapeDtypeStruct((1, 64), F32),
            jax.ShapeDtypeStruct((64, 1024), F32),
            jax.ShapeDtypeStruct((64, 1024), F32),
        ),
        in_specs=[hbm] * 3,
        out_specs=(hbm,) * 3,
        scratch_shapes=[pltpu.VMEM((1, 64), F32), pltpu.VMEM((2, 64, 1024), F32), dma((2, 5))],
    )(loss, vgrad, tgrad)
    return loss.reshape(64), vgrad, tgrad


def solution(mesh):
    return jax.shard_map(
        shards,
        mesh=mesh,
        in_specs=(P(("row", "col"), None), P(("row", "col"), None), P(("row", "col")), P(), P()),
        out_specs=(P(("row", "col")), P(("row", "col"), None), P(("row", "col"), None)),
        check_vma=False,
    )
```

```python
import jax
import jax.numpy as jnp
from jax import lax
from jax.experimental import pallas as pl
from jax.experimental.pallas import tpu as pltpu
from jax.sharding import PartitionSpec as P

EPS = 1e-06
MESH = pl.DeviceIdType.MESH
F32 = jnp.float32
BF16 = jnp.bfloat16
F8 = jnp.float8_e4m3fn


OWN = -1


def make_source():
    source = {}
    for way in range(4):
        first, part = way // 2, way % 2
        across = (2, 3) if first == 0 else (0, 1)
        for k in range(2):
            source[way, k] = (OWN, first, k)
            source[way, 2 + k] = (OWN, 1 - first, k)
        source[way, 4] = (way, part)
        source[way, 5] = (across[0], 0)
        source[way, 6] = (across[1], 0)
        source[way, 7] = (across[0], 1)
        source[way, 8] = (across[1], 1)
        source[way, 9] = (way, 2 + part)
        source[way, 10] = (across[0], 4)
        source[way, 11] = (across[1], 4)
        source[way, 12] = (way, 7 if part else 5)
        source[way, 13] = (way, 8 if part else 6)
        source[way, 14] = (way, 11 if part else 10)
    return source


SOURCE = make_source()


def children(slot):
    return [key for key, value in sorted(SOURCE.items(), key=lambda item: item[0][1]) if value == slot]


def identity(slot):
    if slot[0] == OWN:
        return (0, 0, slot[1], slot[2])
    dx, dy, half, part = identity(SOURCE[slot])
    step = 1 if slot[0] % 2 else 3
    if slot[0] < 2:
        return ((dx + step) % 4, dy, half, part)
    return (dx, (dy + step) % 4, half, part)


def video_row(hg, half, way, who):
    if isinstance(hg, int) and hg == 3:
        return 896 * way + 64 * half + 32 * who
    return 128 + 256 * hg + 128 * half + 64 * way + 32 * who


def text_row(slot):
    if slot[0] == OWN:
        return 32 * slot[1] + 16 * slot[2]
    return 64 * (slot[1] + 1) + 16 * slot[0]


def dot_nn(a, b):
    return lax.dot_general(a, b, (((1,), (0,)), ((), ())), preferred_element_type=F32)


def dot_nt(a, b):
    return lax.dot_general(a, b, (((1,), (1,)), ((), ())), preferred_element_type=F32)


def dot_tn(a, b):
    return lax.dot_general(a, b, (((0,), (0,)), ((), ())), preferred_element_type=F32)


def split(x):
    hi = x.astype(BF16)
    return hi, x - hi.astype(F32)


HI8, LO8 = 2.0**8, 2.0**17
W_HI8, W_LO8 = 2.0**4, 2.0**13


def rows(start, size):
    if not isinstance(start, int):
        start = pl.multiple_of(start, size)
    return pl.ds(start, size)


def kernel(
    video_any, text_any, ids_any, log_scale_any, bias_any,
    loss_ref, vgrad_ref, tgrad_ref,
    vf, tf, vh, v8, th, t8, dots, w, w8, vg, tg, recv_t, recv_v, recv_s, ids_all, ids_own, ids_vec, vidx, lacc, lrow, lrecv, inv_v, inv_t, video_ref, text_ref, ids_ref, log_scale_ref, bias_ref,
    t_send, t_recv, z_send, z_recv, s_send, s_recv, i_send, i_recv,
    rt_send, rt_recv, rz_send, rz_recv, rs_send, rs_recv, l_send, l_recv, in_sem,
):
    row, col = lax.axis_index("row"), lax.axis_index("col")
    z, x, y, core = row // 4, row % 4, col // 2, col % 2

    def at(x_, y_, z_, core_):
        return (z_ * 4 + x_, y_ * 2 + core_)

    xp, xm, yp, ym = (x + 1) % 4, (x + 3) % 4, (y + 1) % 4, (y + 3) % 4
    t_out = (at(xp, y, z, core), at(xm, y, z, core), at(x, yp, z, core), at(x, ym, z, core))
    t_back = (t_out[1], t_out[0], t_out[3], t_out[2])
    line_x = tuple(at((x + d) % 4, y, z, core) for d in range(4))
    line_y = tuple(at(x, (y + d) % 4, z, core) for d in range(4))
    z_out = (at(x, y, (z + 1) % 8, core), at(x, y, (z + 7) % 8, core))
    z_back = (z_out[1], z_out[0])
    other = at(x, y, z, 1 - core)

    loads = [
        pltpu.make_async_copy(src, dst, in_sem.at[n])
        for n, (src, dst) in enumerate(
            (
                (text_any, text_ref), (video_any, video_ref), (ids_any, ids_ref),
                (log_scale_any, log_scale_ref), (bias_any, bias_ref),
            )
        )
    ]
    for load in loads:
        load.start()

    barrier = pltpu.get_barrier_semaphore()
    for peer in line_x[1:] + line_y[1:]:
        pl.semaphore_signal(barrier, inc=1, device_id=peer, device_id_type=MESH)
    pl.semaphore_signal(barrier, inc=1, device_id=other, device_id_type=MESH)
    for peer in z_out:
        pl.semaphore_signal(barrier, inc=1, device_id=peer, device_id_type=MESH)

    def unit(ref, inv_ref):
        full = ref[...]
        inv = lax.rsqrt(jnp.sum(full * full, axis=1, keepdims=True) + EPS)
        inv_ref[...] = jnp.broadcast_to(inv, (64, 128))
        return full * inv

    loads[0].wait()
    tu = unit(text_ref, inv_t)
    tf[rows(0, 64), :] = tu
    loads[1].wait()
    vu = unit(video_ref, inv_v)
    for half in range(2):
        vf[rows(64 * half, 32), :] = vu[32 * half : 32 * half + 32]
    lane = lax.broadcasted_iota(jnp.int32, (1, 128), 1)
    loads[2].wait()
    for quarter in range(4):
        vec = jnp.zeros((1, 128), jnp.int32)
        for n in range(16):
            vec = jnp.where(lane % 16 == n, ids_ref[16 * quarter + n], vec)
        ids_own[quarter : quarter + 1, :] = vec

    def t_copy(slot):
        way, tick = slot
        return pltpu.make_async_remote_copy(
            src_ref=tf.at[rows(text_row(SOURCE[slot]), 16)], dst_ref=tf.at[rows(text_row(slot), 16)],
            send_sem=t_send.at[way], recv_sem=t_recv.at[way, tick],
            device_id=t_out[way], device_id_type=MESH,
        )

    def v_slot(tick, way):
        q = tick % 4
        return 128 + 256 * (tick // 4) + 128 * (q // 2) + 64 * way + 16 * (q % 2)

    def z_copy(way, tick, src, dst):
        return pltpu.make_async_remote_copy(
            src_ref=vf.at[rows(src, 16)], dst_ref=vf.at[rows(dst, 16)],
            send_sem=z_send.at[way], recv_sem=z_recv.at[way, tick],
            device_id=z_out[way], device_id_type=MESH,
        )

    def s_copy(way, tick, src):
        return pltpu.make_async_remote_copy(
            src_ref=vf.at[rows(src, 16)], dst_ref=vf.at[rows(src + 32, 16)],
            send_sem=s_send.at[way], recv_sem=s_recv.at[way, tick],
            device_id=other, device_id_type=MESH,
        )

    def ix_copy(d):
        return pltpu.make_async_remote_copy(
            src_ref=ids_own, dst_ref=ids_all.at[0, (4 - d) % 4],
            send_sem=i_send.at[0], recv_sem=i_recv.at[0, (4 - d) % 4],
            device_id=line_x[d], device_id_type=MESH,
        )

    def iy_copy(d):
        return pltpu.make_async_remote_copy(
            src_ref=ids_all.at[0], dst_ref=ids_all.at[(4 - d) % 4],
            send_sem=i_send.at[1], recv_sem=i_recv.at[1, (4 - d) % 4],
            device_id=line_y[d], device_id_type=MESH,
        )

    pl.semaphore_wait(barrier, 9)

    for d in range(1, 4):
        ix_copy(d).start()
    ids_all[0, 0] = ids_own[...]
    for part in range(2):
        for way in range(2):
            for q in (2 * part, 2 * part + 1):
                z_copy(way, q, 64 * (q // 2) + 16 * (q % 2), v_slot(q, way)).start()
        for way in range(4):
            t_copy((way, part)).start()
    for k in range(2, 4):
        for way in range(4):
            t_copy((way, k)).start()
    for q in range(4):
        s_copy(q // 2, 14 + q % 2, 64 * (q // 2) + 16 * (q % 2)).start()

    local = lax.broadcasted_iota(jnp.int32, (32, 128), 0)
    for hg in range(4):
        for half in range(2):
            for way in range(2):
                for who in range(2):
                    if hg < 3:
                        from_z = (z + (7 - hg if way == 0 else hg + 1)) % 8
                    else:
                        from_z = (z + 4 * way) % 8
                    from_core = core if who == 0 else 1 - core
                    base = ((from_z * 4 + x) * 8 + y * 2 + from_core) * 64 + 32 * half
                    vidx[rows(video_row(hg, half, way, who), 32), :] = local + base
    lacc[...] = jnp.zeros_like(lacc)

    loads[3].wait()
    loads[4].wait()
    scale = jnp.exp(jnp.full((1, 128), log_scale_ref[0], F32))
    bias = jnp.full((1, 128), bias_ref[0], F32)

    def t_split(start, size):
        full = tf[rows(start, size), :]
        hi, lo = split(full)
        th[rows(start, size), :] = hi
        t8[0, rows(start, size), :] = (lo * LO8).astype(F8)
        t8[1, rows(start, size), :] = (full * HI8).astype(F8)

    def v_split(start, size):
        full = vf[rows(start, size), :]
        hi, lo = split(full)
        vh[rows(start, size), :] = hi
        v8[0, rows(start, size), :] = (full * HI8).astype(F8)
        v8[1, rows(start, size), :] = (lo * LO8).astype(F8)

    def place(n):
        if isinstance(n, int):
            m = int(n**0.5)
            r = n - m * m
            return (r, m) if r <= m else (m, r - m - 1)
        m = (n >= 1).astype(jnp.int32) + (n >= 4).astype(jnp.int32) + (n >= 9).astype(jnp.int32)
        r = n - m * m
        return jnp.where(r <= m, r, m), jnp.where(r <= m, m, r - m - 1)

    def some_dots(start, size, tb):
        vs, ts = rows(start, size), rows(tb * 256, 256)
        small = dot_nt(
            jnp.concatenate([v8[0, vs, :], v8[1, vs, :]], axis=1), jnp.concatenate([t8[0, ts, :], t8[1, ts, :]], axis=1)
        )
        dots[:size, :] = dot_nt(vh[vs, :], th[ts, :]) + small * (1.0 / (HI8 * LO8))

    def some_rest(start, size, tb):
        vs = rows(start, size)
        es = []
        for half in range(2):
            logits = dots[:size, 128 * half : 128 * half + 128] * scale + bias
            match = vidx[vs, :] == ids_vec[tb * 2 + half]
            e = jnp.exp(jnp.where(match, -logits, logits))
            es.append(e)
            weight = (jnp.where(match, -scale, scale) * e) / (1.0 + e)
            hi, lo = split(weight)
            hi8, lo8 = (weight * W_HI8).astype(F8), (lo * W_LO8).astype(F8)
            cols = rows((tb * 2 + half) * 128, 128)
            for k in range(size // 128):
                w[start // 128 + k, :, cols] = hi[128 * k : 128 * k + 128]
                w8[0, start // 128 + k, :, cols] = hi8[128 * k : 128 * k + 128]
                w8[1, start // 128 + k, :, cols] = lo8[128 * k : 128 * k + 128]
        both = es[0] + es[1] + es[0] * es[1]
        small = both * (1.0 - both * (0.5 - both * (1.0 / 3.0)))
        lacc[vs, :] += jnp.where(both < 1.0 / 64.0, small, jnp.log(1.0 + both))

    def block_dots(n):
        vb, tb = place(n)
        some_dots(vb * 256, 256, tb)

    def block_rest(n):
        vb, tb = place(n)
        some_rest(vb * 256, 256, tb)

    def group_ids(group):
        vec = jnp.zeros((1, 128), jnp.int32)
        for spot in range(8):
            if spot >= 4:
                slot = (spot - 4, 2 * group)
            elif group > 0:
                slot = (spot, 2 * group - 1)
            else:
                slot = (OWN, spot // 2, spot % 2)
            dx, dy, half, part = identity(slot)
            ids = ids_all[dy, dx, pl.ds(2 * half + part, 1), :]
            vec = ids if spot == 0 else jnp.where(lane < 16 * spot, vec, ids)
        return vec

    def count(tick):
        done = 0
        for bound, more in ((2, 1), (6, 1), (7, 1), (8, 1), (10, 2), (11, 1), (12, 1), (13, 1)):
            done = done + jnp.where(tick >= bound, more, 0)
        return done

    @pl.loop(0, 15)
    def _(tick):
        for way in range(2):

            @pl.when(tick < 12)
            def _():
                slot = v_slot(tick, way)
                z_copy(way, tick, slot, slot).wait_recv()

                @pl.when(tick < 8)
                def _():
                    z_copy(way, tick + 4, slot, slot + 256).start()

                @pl.when((tick >= 8) & ((tick % 4) // 2 == way))
                def _():
                    last = 896 + 64 * way + 16 * (tick % 2)
                    z_copy(way, 12 + tick % 2, slot, last).start()

                s_copy(way, tick, slot).start()

            @pl.when((tick == 12) | (tick == 13))
            def _():
                slot = 896 + 64 * way + 16 * (tick % 2)
                z_copy(way, tick, slot, slot).wait_recv()
                s_copy(way, tick, slot).start()

            @pl.when((tick >= 1) & (tick <= 12))
            def _():
                s_copy(way, tick - 1, v_slot(tick - 1, way)).wait_recv()

            @pl.when(tick == 13)
            def _():
                s_copy(way, tick - 1, 896 + 64 * way + 16 * ((tick - 1) % 2)).wait_recv()

            @pl.when(tick == 1)
            def _():
                for part in range(2):
                    s_copy(way, 14 + part, 64 * way + 16 * part).wait_recv()

        for k in range(15):

            @pl.when(tick == k)
            def _():
                for way in range(4):
                    t_copy((way, k)).wait_recv()
                    for child in children((way, k)):
                        t_copy(child).start()
                if k == 0:
                    for d in range(1, 4):
                        ix_copy(d).wait_recv()
                    for d in range(1, 4):
                        iy_copy(d).start()
                if k == 3:
                    for d in range(1, 4):
                        iy_copy(d).wait_recv()
                    for group in range(8):
                        ids_vec[group] = group_ids(group)

        @pl.when(tick % 2 == 0)
        def _():
            t_split(64 * tick, 128)

        @pl.when((tick == 1) | ((tick % 2 == 0) & (tick >= 2) & (tick <= 12)))
        def _():
            v_split(jnp.where(tick == 1, 0, 64 * tick), 128)

        @pl.when(tick == 2)
        def _():
            block_dots(0)

        @pl.loop(jnp.maximum(count(tick - 1), 1), count(tick))
        def _(n):
            block_rest(n - 1)
            block_dots(n)

        @pl.when(tick == 13)
        def _():
            block_rest(8)
            for way in range(2):
                s_copy(way, 13, 896 + 64 * way + 16).wait_recv()
            v_split(896, 128)
            block_dots(13)
            block_rest(13)

    @pl.loop(0, 1)
    def _(n):
        some_dots(n * 1024, 1024, 3)
        some_rest(n * 1024, 1024, 3)

    def rt_copy(slot):
        way, tick = slot
        row_ = text_row(slot)
        return pltpu.make_async_remote_copy(
            src_ref=tg.at[rows(row_, 16)], dst_ref=recv_t.at[rows(row_, 16)],
            send_sem=rt_send.at[way], recv_sem=rt_recv.at[way, tick],
            device_id=t_back[way], device_id_type=MESH,
        )

    def t_sum(slot):
        total = tg[rows(text_row(slot), 16), :]
        for child in children(slot):
            rt_copy(child).wait_recv()
            total = total + recv_t[rows(text_row(child), 16), :]
        return total

    def t_pump(tick):
        for way in range(4):
            slot = (way, tick)
            if children(slot):
                tg[rows(text_row(slot), 16), :] = t_sum(slot)
            rt_copy(slot).start()

    def rz_copy(way, half, step, src):
        return pltpu.make_async_remote_copy(
            src_ref=vg.at[rows(src, 32)], dst_ref=recv_v.at[step, half, way],
            send_sem=rz_send.at[way], recv_sem=rz_recv.at[way, half, step],
            device_id=z_back[way], device_id_type=MESH,
        )

    def rs_copy(hg, half, way):
        return pltpu.make_async_remote_copy(
            src_ref=vg.at[rows(video_row(hg, half, way, 1), 32)], dst_ref=recv_s.at[hg, half, way],
            send_sem=rs_send.at[0], recv_sem=rs_recv.at[hg, half, way],
            device_id=other, device_id_type=MESH,
        )

    def z_pump(hg, half, with_recv):
        for way in range(2):
            slot = video_row(hg, half, way, 0)
            rs_copy(hg, half, way).wait_recv()
            if with_recv[way]:
                rz_copy(way, half, hg + 1, slot).wait_recv()
                vg[rows(slot, 32), :] += recv_s[hg, half, way] + recv_v[hg + 1, half, way]
            else:
                vg[rows(slot, 32), :] += recv_s[hg, half, way]
            rz_copy(way, half, hg, slot).start()

    def z_last():
        for half in range(2):
            slot = 896 + 64 * half
            rs_copy(3, half, 1).wait_recv()
            vg[rows(slot, 32), :] += recv_s[3, half, 1]
            rz_copy(half, half, 3, slot).start()

    def t_grad(g):
        cols = pl.ds(pl.multiple_of(g * 128, 128), 128)
        hi = w[:, :, cols].reshape(1024, 128)
        lo8 = w8[1, :, :, cols].reshape(1024, 128)
        hi8 = w8[0, :, :, cols].reshape(1024, 128)
        small = dot_tn(jnp.concatenate([lo8, hi8], axis=0), v8[...].reshape(2048, 1024))
        tg[rows(g * 128, 128), :] = dot_tn(hi, vh[...]) + small * (1.0 / (W_HI8 * LO8))

    def v_grad(m):
        small = dot_nn(jnp.concatenate([w8[0, m], w8[1, m]], axis=1), t8[...].reshape(2048, 1024))
        vg[rows(m * 128, 128), :] = dot_nn(w[m], th[...]) + small * (1.0 / (W_HI8 * LO8))

    def l_copy(hg, way, who, owner):
        slot = (hg * 2 + way) * 2 + who
        return pltpu.make_async_remote_copy(
            src_ref=lrow.at[pl.ds(1 + 2 * hg if hg < 3 else 6 * way, 2)], dst_ref=lrecv.at[slot],
            send_sem=l_send.at[0], recv_sem=l_recv.at[slot],
            device_id=owner, device_id_type=MESH,
        )

    def l_peers():
        peers = []
        for hg in range(4):
            for way in range(2):
                if hg < 3:
                    to_z = (z + (7 - hg if way == 0 else hg + 1)) % 8
                else:
                    to_z = (z + 4 * way) % 8
                for who in range(2):
                    if (hg, way, who) != (3, 0, 0):
                        peers.append((hg, way, who, at(x, y, to_z, core if who == 0 else 1 - core)))
        return peers

    t_grad(7)
    t_pump(14)
    t_pump(13)

    @pl.loop(14, 16)
    def _(n):
        block_dots(n)
        block_rest(n)

    @pl.loop(0, 7)
    def _(i):
        hg, half = 2 - (i - 1) // 2, (i - 1) % 2
        v_grad(jnp.where(i == 0, 7, 1 + 2 * hg + half))

        @pl.when(i == 0)
        def _():
            for half_ in range(2):
                rs_copy(3, half_, 1).start()

        @pl.when(i > 0)
        def _():
            for way in range(2):
                rs_copy(hg, half, way).start()

        t_grad(6 - i)
        @pl.when(i == 0)
        def _():
            z_last()

        @pl.when(i == 1)
        def _():
            z_pump(2, 0, (True, False))

        @pl.when(i == 2)
        def _():
            z_pump(2, 1, (False, True))

        @pl.when(i >= 3)
        def _():
            z_pump(hg, half, (True, True))

        for k in range(7):

            @pl.when(i == k)
            def _():
                t_pump(12 - 2 * k)
                if k < 6:
                    t_pump(11 - 2 * k)

        @pl.when(i == 3)
        def _():
            ones = jnp.ones((16, 128), BF16)
            hi, lo = split(lacc[...])
            sums = dot_nt(ones, hi) + dot_nt(ones, lo.astype(BF16))
            for m in range(8):
                lrow[m] = sums[:1, 128 * m : 128 * m + 128]
            for hg_, way, who, owner in l_peers():
                l_copy(hg_, way, who, owner).start()

    v_grad(0)
    for half in range(2):
        rs_copy(3, half, 0).start()

    loss = [lrow[0, :, 64 * half : 64 * half + 32] for half in range(2)]
    for hg, way, who, owner in l_peers():
        l_copy(hg, way, who, owner).wait_recv()
        part = lrecv.at[(hg * 2 + way) * 2 + who]
        for half in range(2):
            if hg < 3:
                first = 64 * way + 32 * who
                loss[half] = loss[half] + part[half, :, first : first + 32]
            else:
                first = 64 * half + 32 * who
                loss[half] = loss[half] + part[way, :, first : first + 32]
    loss_ref[:, :32] = loss[0]
    loss_ref[:, 32:] = loss[1]

    for half in range(2):
        for part in range(2):
            own = text_row((OWN, half, part))
            total = t_sum((OWN, half, part))
            u = tf[rows(own, 16), :]
            first = 32 * half + 16 * part
            back = total - u * jnp.sum(u * total, axis=1, keepdims=True)
            tgrad_ref[rows(first, 16), :] = back * inv_t[rows(first, 16), :1]

    for half in range(2):
        own = 64 * half
        rs_copy(3, half, 0).wait_recv()
        total = vg[rows(own, 32), :] + recv_s[3, half, 0]
        for way in range(2):
            rz_copy(way, half, 0, own).wait_recv()
            total = total + recv_v[0, half, way]
        u = vf[rows(own, 32), :]
        back = total - u * jnp.sum(u * total, axis=1, keepdims=True)
        vgrad_ref[rows(32 * half, 32), :] = back * inv_v[rows(32 * half, 32), :1]

    def drain(ref, sem):
        pltpu.make_async_remote_copy(
            src_ref=ref, dst_ref=ref, send_sem=sem, recv_sem=sem, device_id=other, device_id_type=MESH
        ).wait_send()

    for way in range(4):
        drain(tf.at[rows(0, 240)], t_send.at[way])
        drain(tg.at[rows(0, 240)], rt_send.at[way])
    for way in range(2):
        drain(vf.at[rows(0, 224)], z_send.at[way])
        drain(vf.at[rows(0, 256)], s_send.at[way])
        drain(vg.at[rows(0, 224)], rz_send.at[way])
    drain(ids_all.at[0, pl.ds(0, 3)], i_send.at[0])
    drain(ids_all.at[pl.ds(0, 3)], i_send.at[1])
    drain(vg.at[rows(0, 512)], rs_send.at[0])
    drain(lrecv.at[pl.ds(0, 15)], l_send.at[0])


def hand_on(loss_any, vgrad_any, tgrad_any, loss_out, vgrad_out, tgrad_out, loss, grads, sems):
    pieces = [(loss_any, loss, loss_out)]
    for n, (src, dst) in enumerate(((vgrad_any, vgrad_out), (tgrad_any, tgrad_out))):
        for part in range(2):
            here = pl.ds(32 * part, 32)
            pieces.append((src.at[here], grads.at[n, here], dst.at[here]))
    first = [pltpu.make_async_copy(a, b, sems.at[0, n]) for n, (a, b, _) in enumerate(pieces)]
    second = [pltpu.make_async_copy(b, c, sems.at[1, n]) for n, (_, b, c) in enumerate(pieces)]
    for copy in first:
        copy.start()
    for come, go in zip(first, second):
        come.wait()
        go.start()
    for copy in second:
        copy.wait()


def shards(video, text, match_ids, log_scale, bias):
    vmem = pl.BlockSpec(memory_space=pltpu.VMEM)
    hbm = pl.BlockSpec(memory_space=pl.ANY)
    dma = pltpu.SemaphoreType.DMA
    loss, vgrad, tgrad = pl.pallas_call(
        kernel,
        out_shape=(
            jax.ShapeDtypeStruct((1, 64), F32),
            jax.ShapeDtypeStruct((64, 1024), F32),
            jax.ShapeDtypeStruct((64, 1024), F32),
        ),
        in_specs=[hbm] * 5,
        out_specs=(vmem, vmem, vmem),
        scratch_shapes=[
            pltpu.VMEM((1024, 1024), F32),
            pltpu.VMEM((1024, 1024), F32),
            pltpu.VMEM((1024, 1024), BF16),
            pltpu.VMEM((2, 1024, 1024), F8),
            pltpu.VMEM((1024, 1024), BF16),
            pltpu.VMEM((2, 1024, 1024), F8),
            pltpu.VMEM((1024, 256), F32),
            pltpu.VMEM((8, 128, 1024), BF16),
            pltpu.VMEM((2, 8, 128, 1024), F8),
            pltpu.VMEM((1024, 1024), F32),
            pltpu.VMEM((1024, 1024), F32),
            pltpu.VMEM((1024, 1024), F32),
            pltpu.VMEM((4, 2, 2, 32, 1024), F32),
            pltpu.VMEM((4, 2, 2, 32, 1024), F32),
            pltpu.VMEM((4, 4, 4, 128), jnp.int32),
            pltpu.VMEM((4, 128), jnp.int32),
            pltpu.VMEM((8, 1, 128), jnp.int32),
            pltpu.VMEM((1024, 128), jnp.int32),
            pltpu.VMEM((1024, 128), F32),
            pltpu.VMEM((8, 1, 128), F32),
            pltpu.VMEM((16, 2, 1, 128), F32),
            pltpu.VMEM((64, 128), F32),
            pltpu.VMEM((64, 128), F32),
            pltpu.VMEM((64, 1024), F32),
            pltpu.VMEM((64, 1024), F32),
            pltpu.SMEM((64,), jnp.int32),
            pltpu.SMEM((1,), F32),
            pltpu.SMEM((1,), F32),
            dma((4,)), dma((4, 15)),
            dma((2,)), dma((2, 14)),
            dma((2,)), dma((2, 16)),
            dma((2,)), dma((2, 4)),
            dma((4,)), dma((4, 15)),
            dma((2,)), dma((2, 2, 4)),
            dma((1,)), dma((4, 2, 2)),
            dma((1,)), dma((16,)), dma((5,)),
        ],
        compiler_params=pltpu.CompilerParams(
            collective_id=0, has_side_effects=True, vmem_limit_bytes=56 * 2**20
        ),
        cost_estimate=pl.CostEstimate(flops=18 * 2**30, bytes_accessed=2**20, transcendentals=3 * 2**20),
    )(video, text, match_ids, log_scale, bias)
    loss, vgrad, tgrad = pl.pallas_call(
        hand_on,
        out_shape=(
            jax.ShapeDtypeStruct((1, 64), F32),
            jax.ShapeDtypeStruct((64, 1024), F32),
            jax.ShapeDtypeStruct((64, 1024), F32),
        ),
        in_specs=[hbm] * 3,
        out_specs=(hbm,) * 3,
        scratch_shapes=[pltpu.VMEM((1, 64), F32), pltpu.VMEM((2, 64, 1024), F32), dma((2, 5))],
    )(loss, vgrad, tgrad)
    return loss.reshape(64), vgrad, tgrad


def solution(mesh):
    return jax.shard_map(
        shards,
        mesh=mesh,
        in_specs=(P(("row", "col"), None), P(("row", "col"), None), P(("row", "col")), P(), P()),
        out_specs=(P(("row", "col")), P(("row", "col"), None), P(("row", "col"), None)),
        check_vma=False,
    )
```
